32 devices in a mesh: gx: 4 (over z), gy: 4 (over y, x), gz: 2 (over core).
Axes of the slice: x: 2, y: 2, z: 4, core: 2. Of those that a mesh axis runs over, the one named last changes fastest.
Arguments:
- bin_mass: float32 [4, 4, 12, 8, 8, 8, 128], P('gx', 'gy', 'gz'), may hold values from 0.1 to 1
- wind_field: float32 [4, 4, 12, 2, 8, 64], P('gx', 'gy', 'gz'), may hold values from -0.3 to 0.3
- fall_speed: float32 [128], replicated, may hold values from 0.02 to 0.4
- gain_a: float32 [128, 128], replicated, may hold values from -0.5 to 0.5
- gain_b: float32 [128, 128], replicated, may hold values from -0.5 to 0.5
- gain_c: float32 [128, 128], replicated, may hold values from -0.5 to 0.5
- loss_k: float32 [128, 128], replicated, may hold values from -0.5 to 0.5
- old_occupied: int32 [4, 4, 6], P('gx', 'gy'), may hold values from 0 to 1, as said below
- old_neighbours: int32 [4, 4, 6, 4], P('gx', 'gy'), may hold values from -1 to 8, as said below
- old_sends: int32 [4, 4, 4, 3], P('gx', 'gy'), may hold values from -1 to 5, as said below
- old_substeps: int32 [1, 4, 4, 12], P(None, 'gx', 'gy', 'gz'), may hold values from 1 to 4
- move_lists: int32 [4, 4, 3, 2], P('gx', 'gy'), may hold values from -1 to 5, as said below
- new_sources: int32 [4, 4, 6], P('gx', 'gy'), may hold values from -1 to 11, as said below
- new_neighbours: int32 [4, 4, 6, 4], P('gx', 'gy'), may hold values from -1 to 8, as said below
- new_sends: int32 [4, 4, 4, 3], P('gx', 'gy'), may hold values from -1 to 5, as said below
- new_substeps: int32 [1, 4, 4, 12], P(None, 'gx', 'gy', 'gz'), may hold values from 1 to 4
Outputs:
- final_mass: float32 [4, 4, 12, 8, 8, 8, 128], P('gx', 'gy', 'gz')
The draws below stay inside these ranges and needn't reach their ends.
Inputs may be any that keep to these rules, and one draw needn't show every extreme that they name: `old_occupied`: slots marked 1 hold blocks before the move; some position has all 6 marked. `old_neighbours`: -1 marks the domain's edge or an empty slot; a value under 6 is a slot of the same device; a value 6 + k is entry k of the list that the device next on that side keeps for the opposite side. Lists before and after the move are consistent with each other and with the send lists. `old_sends`: entries are occupied slots of the device, -1 pads; some list holds 3 entries. `move_lists`: entries are occupied old slots, each block sent at most once, -1 pads; routes 0 and 1 each hold 2 entries on some device. `new_sources`: -1 marks an empty slot; a value under 6 is an own old slot that stays; 6 + r * 2 + k is entry k of route r of the sending device; every block has exactly one new slot. `new_neighbours`: as old_neighbours, for the layout after the move. `new_sends`: as old_sends, for the layout after the move.
All inputs are finite; a program needn't handle non-finite values.
Results may differ from the reference program's by a relative error of at most 0.0003.
Values sent between devices are 32-bit elements; how exact they have to be, the bound alone decides.
A program may use at most 64 MiB of HBM per device.

```python
import math
import jax
import jax.numpy as jnp
from jax import lax

BINS = 128
BX = 8
BY = 8
BZ = 8
TX = 2
TY = 2
SMAX = 4
HALF_STEPS = 1
SLOTS = 6
FCAP = 3
MCAP = 2
N_GX = 4
N_GY = 4
N_GZ = 2


def relabel_codes(codes, rank):
    flat = codes.reshape(N_GX, N_GY, -1)
    mapped = jnp.take_along_axis(rank, jnp.clip(flat, 0, SLOTS - 1), axis=2)
    return jnp.where((flat >= 0) & (flat < SLOTS), mapped, flat).reshape(codes.shape).astype(jnp.int32)


def layout_lists(key):
    key_x, key_y, key_p, key_q = jax.random.split(jax.random.fold_in(key, 7), 4)
    col_index = jnp.arange(N_GX, dtype=jnp.int32)
    row_index = jnp.arange(N_GY, dtype=jnp.int32)
    mid_x = N_GX // 2
    mid_y = N_GY // 2
    force_x = (col_index == 0) | (col_index == mid_x) | (col_index == N_GX - 2) | (col_index == mid_x - 1) & (N_GX > 4)
    force_y = (row_index == 0) | (row_index == mid_y - 1) | (row_index == mid_y) | (row_index == N_GY - 2) | (row_index == mid_y - 2) & (N_GY > 4)
    move_x = jax.random.randint(key_x, (N_GX,), 0, 2).astype(jnp.int32)
    move_x = jnp.where(col_index == N_GX - 1, 0, jnp.where(force_x, 1, move_x))
    move_y = jax.random.randint(key_y, (N_GY,), 0, 2).astype(jnp.int32)
    move_y = jnp.where(row_index == N_GY - 1, 0, jnp.where(force_y, 1, move_y))
    prev_x = jnp.concatenate([jnp.zeros((1,), jnp.int32), move_x[:-1]])
    prev_y = jnp.concatenate([jnp.zeros((1,), jnp.int32), move_y[:-1]])
    width_cols = TX + prev_x - move_x
    height = TY + prev_y - move_y
    full_shape = (N_GX, N_GY, SLOTS)
    dev_i = jnp.broadcast_to(col_index[:, None, None], full_shape)
    dev_j = jnp.broadcast_to(row_index[None, :, None], full_shape)
    slot_index = jnp.broadcast_to(jnp.arange(SLOTS, dtype=jnp.int32)[None, None, :], full_shape)
    width_dev = width_cols[dev_i]
    height_dev = height[dev_j]
    col_a = slot_index // TY
    row_r = slot_index % TY
    old_live = slot_index < width_dev * TY
    west_code = jnp.where(col_a > 0, slot_index - TY, jnp.where(dev_i == 0, -1, SLOTS + row_r))
    east_code = jnp.where(col_a < width_dev - 1, slot_index + TY, jnp.where(dev_i == N_GX - 1, -1, SLOTS + row_r))
    south_code = jnp.where(row_r > 0, slot_index - 1, jnp.where(dev_j == 0, -1, SLOTS + col_a))
    north_code = jnp.where(row_r < TY - 1, slot_index + 1, jnp.where(dev_j == N_GY - 1, -1, SLOTS + col_a))
    old_neighbours = jnp.where(old_live[..., None], jnp.stack([west_code, east_code, south_code, north_code], axis=-1), -1).astype(jnp.int32)
    send_shape = (N_GX, N_GY, FCAP)
    entry_index = jnp.broadcast_to(jnp.arange(FCAP, dtype=jnp.int32)[None, None, :], send_shape)
    at_i = jnp.broadcast_to(col_index[:, None, None], send_shape)
    at_j = jnp.broadcast_to(row_index[None, :, None], send_shape)
    wide_cols = width_cols[at_i]
    tall_rows = height[at_j]
    send_west = jnp.where((entry_index < TY) & (at_i > 0), entry_index, -1)
    send_east = jnp.where((entry_index < TY) & (at_i < N_GX - 1), (wide_cols - 1) * TY + entry_index, -1)
    send_south = jnp.where((entry_index < wide_cols) & (at_j > 0), entry_index * TY, -1)
    send_north = jnp.where((entry_index < wide_cols) & (at_j < N_GY - 1), entry_index * TY + TY - 1, -1)
    old_sends = jnp.stack([send_west, send_east, send_south, send_north], axis=2).astype(jnp.int32)
    row_b = slot_index // TX
    col_c = slot_index % TX
    new_live = slot_index < height_dev * TX
    west_code = jnp.where(col_c > 0, slot_index - 1, jnp.where(dev_i == 0, -1, SLOTS + row_b))
    east_code = jnp.where(col_c < TX - 1, slot_index + 1, jnp.where(dev_i == N_GX - 1, -1, SLOTS + row_b))
    south_code = jnp.where(row_b > 0, slot_index - TX, jnp.where(dev_j == 0, -1, SLOTS + col_c))
    north_code = jnp.where(row_b < height_dev - 1, slot_index + TX, jnp.where(dev_j == N_GY - 1, -1, SLOTS + col_c))
    new_neighbours = jnp.where(new_live[..., None], jnp.stack([west_code, east_code, south_code, north_code], axis=-1), -1).astype(jnp.int32)
    send_west = jnp.where((entry_index < tall_rows) & (at_i > 0), entry_index * TX, -1)
    send_east = jnp.where((entry_index < tall_rows) & (at_i < N_GX - 1), entry_index * TX + TX - 1, -1)
    send_south = jnp.where((entry_index < TX) & (at_j > 0), entry_index, -1)
    send_north = jnp.where((entry_index < TX) & (at_j < N_GY - 1), (tall_rows - 1) * TX + entry_index, -1)
    new_sends = jnp.stack([send_west, send_east, send_south, send_north], axis=2).astype(jnp.int32)
    block_x = dev_i * TX - prev_x[dev_i] + col_a
    block_y = dev_j * TY + row_r
    tile_x = jnp.clip(block_x // TX, 0, N_GX - 1)
    move_bx = (move_x[tile_x] == 1) & (block_x % TX == TX - 1)
    move_by = (move_y[dev_j] == 1) & (row_r == TY - 1)
    route_dir = jnp.where(move_bx & move_by, 2, jnp.where(move_bx, 0, jnp.where(move_by, 1, 3)))
    route_dir = jnp.where(old_live, route_dir, 3).astype(jnp.int32)
    route_hot = (route_dir[..., None] == jnp.arange(4, dtype=jnp.int32)[None, None, None, :]).astype(jnp.int32)
    route_rank = jnp.sum((jnp.cumsum(route_hot, axis=2) - route_hot) * route_hot, axis=-1).astype(jnp.int32)
    full_lists = jnp.full((N_GX, N_GY, 4, SLOTS), -1, jnp.int32).at[dev_i, dev_j, route_dir, route_rank].set(slot_index)
    move_lists = full_lists[:, :, :3, :MCAP]
    dest_j = jnp.clip(dev_j + move_by.astype(jnp.int32), 0, N_GY - 1)
    low_y = dest_j * TY - prev_y[dest_j]
    dest_slot = jnp.where(old_live, (block_y - low_y) * TX + (block_x - tile_x * TX), SLOTS).astype(jnp.int32)
    source_code = jnp.where(route_dir == 3, slot_index, SLOTS + route_dir * MCAP + route_rank).astype(jnp.int32)
    sources = jnp.full((N_GX, N_GY, SLOTS + 1), -1, jnp.int32).at[tile_x, dest_j, dest_slot].set(source_code)
    new_sources = sources[:, :, :SLOTS]
    scores = jax.random.randint(key_p, full_shape, 0, 4096).astype(jnp.int32) * SLOTS + slot_index
    order = jnp.argsort(scores, axis=2).astype(jnp.int32)
    rank = jnp.argsort(order, axis=2).astype(jnp.int32)
    old_neighbours = relabel_codes(old_neighbours, rank)
    old_neighbours = jnp.take_along_axis(old_neighbours, jnp.broadcast_to(order[..., None], old_neighbours.shape), axis=2).astype(jnp.int32)
    old_sends = relabel_codes(old_sends, rank)
    move_lists = relabel_codes(move_lists, rank)
    new_sources = relabel_codes(new_sources, rank)
    old_occupied = jnp.take_along_axis(old_live.astype(jnp.int32), order, axis=2).astype(jnp.int32)
    new_scores = jax.random.randint(key_q, full_shape, 0, 4096).astype(jnp.int32) * SLOTS + slot_index
    new_order = jnp.argsort(new_scores, axis=2).astype(jnp.int32)
    new_rank = jnp.argsort(new_order, axis=2).astype(jnp.int32)
    new_neighbours = relabel_codes(new_neighbours, new_rank)
    new_neighbours = jnp.take_along_axis(new_neighbours, jnp.broadcast_to(new_order[..., None], new_neighbours.shape), axis=2).astype(jnp.int32)
    new_sends = relabel_codes(new_sends, new_rank)
    new_sources = jnp.take_along_axis(new_sources, new_order, axis=2).astype(jnp.int32)
    return (old_occupied, old_neighbours, old_sends, move_lists, new_sources, new_neighbours, new_sends)


def draw_old_occupied(key, part):
    return layout_lists(key)[0]


def draw_old_neighbours(key, part):
    return layout_lists(key)[1]


def draw_old_sends(key, part):
    return layout_lists(key)[2]


def draw_move_lists(key, part):
    return layout_lists(key)[3]


def draw_new_sources(key, part):
    return layout_lists(key)[4]


def draw_new_neighbours(key, part):
    return layout_lists(key)[5]


def draw_new_sends(key, part):
    return layout_lists(key)[6]


def touch_ends(entries, own_key, smallest, top_value):
    place = [jax.random.randint(jax.random.fold_in(own_key, axis), (), 0, length) for axis, length in enumerate(entries.shape)]
    main_axis = entries.shape.index(max(entries.shape))
    beside = place[:main_axis] + [(place[main_axis] + 1) % entries.shape[main_axis]] + place[main_axis + 1:]
    return entries.at[tuple(place)].set(smallest).at[tuple(beside)].set(top_value)


def steps_of(own_key, extent, shards, least, high):
    factor_of, own = 1.0, jax.random.fold_in(own_key, 6)
    for dim, shards_of in shards:
        steps = jnp.exp(jax.random.uniform(jax.random.fold_in(own, dim), (shards_of,), jnp.float32, least / len(shards), high / len(shards)))
        factor_of = factor_of * jnp.repeat(steps, extent[dim] // shards_of).reshape([-1 if axis == dim else 1 for axis in range(len(extent))])
    return factor_of


def scatter_about(key, shape, width, bound, held_as=jnp.bfloat16):
    return jnp.clip(width * jax.random.normal(key, shape, jnp.float32), -bound, bound).astype(held_as)


def setup_inputs(seed: int = 0) -> dict:
    keys = jax.random.split(jax.random.key(seed), 17)
    bin_mass = jnp.clip(0.1 + 0.9 * jax.random.uniform(keys[0], (N_GX, N_GY, N_GZ * SLOTS, BX, BY, BZ, BINS), jnp.float32) ** steps_of(keys[0], (N_GX, N_GY, N_GZ * SLOTS, BX, BY, BZ, BINS), ((0, 4), (1, 4), (2, 2)), -0.2, 0.2), 0.1, 1.0)
    wind_field = jnp.clip(jax.random.uniform(keys[1], (N_GX, N_GY, N_GZ * SLOTS, 2, BX, BY * BZ), jnp.float32, -0.3, 0.3) * steps_of(keys[1], (N_GX, N_GY, N_GZ * SLOTS, 2, BX, BY * BZ), ((0, 4), (1, 4), (2, 2)), -0.4, 0.0), -0.3, 0.3)
    fall_speed = jnp.clip(jnp.exp(jax.random.uniform(keys[2], (BINS,), jnp.float32, math.log(0.02), math.log(0.4))), 0.02, 0.4)
    gain_a = scatter_about(keys[3], (BINS, BINS), BINS ** -0.5, 0.5, jnp.float32)
    gain_b = scatter_about(keys[4], (BINS, BINS), BINS ** -0.5, 0.5, jnp.float32)
    gain_c = scatter_about(keys[5], (BINS, BINS), BINS ** -0.5, 0.5, jnp.float32)
    loss_k = scatter_about(keys[6], (BINS, BINS), BINS ** -0.5, 0.5, jnp.float32)
    old_occupied = draw_old_occupied(jax.random.fold_in(keys[16], 71), 0)
    old_neighbours = draw_old_neighbours(jax.random.fold_in(keys[16], 71), 0)
    old_sends = draw_old_sends(jax.random.fold_in(keys[16], 71), 0)
    old_substeps = touch_ends(jax.random.randint(keys[10], (HALF_STEPS, N_GX, N_GY, N_GZ * SLOTS), 1, SMAX + 1), jax.random.fold_in(keys[10], 1), 1, SMAX).astype(jnp.int32)
    move_lists = draw_move_lists(jax.random.fold_in(keys[16], 71), 0)
    new_sources = draw_new_sources(jax.random.fold_in(keys[16], 71), 0)
    new_neighbours = draw_new_neighbours(jax.random.fold_in(keys[16], 71), 0)
    new_sends = draw_new_sends(jax.random.fold_in(keys[16], 71), 0)
    new_substeps = touch_ends(jax.random.randint(keys[15], (HALF_STEPS, N_GX, N_GY, N_GZ * SLOTS), 1, SMAX + 1), jax.random.fold_in(keys[15], 1), 1, SMAX).astype(jnp.int32)
    return dict(bin_mass=bin_mass, wind_field=wind_field, fall_speed=fall_speed, gain_a=gain_a, gain_b=gain_b, gain_c=gain_c, loss_k=loss_k, old_occupied=old_occupied, old_neighbours=old_neighbours, old_sends=old_sends, old_substeps=old_substeps, move_lists=move_lists, new_sources=new_sources, new_neighbours=new_neighbours, new_sends=new_sends, new_substeps=new_substeps)


step_time = 0.25


def coag_tendency(mass_field, gain_a, gain_b, gain_c, loss_k):
    exact_mode = lax.Precision.HIGHEST
    first_map = jnp.matmul(mass_field, gain_a, precision=exact_mode, preferred_element_type=jnp.float32)
    second_map = jnp.matmul(mass_field, gain_b, precision=exact_mode, preferred_element_type=jnp.float32)
    gained = jnp.matmul(first_map * second_map, gain_c, precision=exact_mode, preferred_element_type=jnp.float32)
    lost_mass = mass_field * jnp.matmul(mass_field, loss_k, precision=exact_mode, preferred_element_type=jnp.float32)
    return gained - lost_mass


def advect(mass_field, speed_x, speed_y, west_mass, west_speed, east_mass, east_speed, south_mass, south_speed, north_mass, north_speed, from_above, fall_speed):
    padded_x = jnp.concatenate([west_mass[..., None, :, :, :], mass_field, east_mass[..., None, :, :, :]], axis=-4)
    wind_x = jnp.concatenate([west_speed[..., None, :, :], speed_x, east_speed[..., None, :, :]], axis=-3)[..., None]
    flux_x = jnp.maximum(wind_x[..., :-1, :, :, :], 0.0) * padded_x[..., :-1, :, :, :] + jnp.minimum(wind_x[..., 1:, :, :, :], 0.0) * padded_x[..., 1:, :, :, :]
    padded_y = jnp.concatenate([south_mass[..., :, None, :, :], mass_field, north_mass[..., :, None, :, :]], axis=-3)
    wind_y = jnp.concatenate([south_speed[..., :, None, :], speed_y, north_speed[..., :, None, :]], axis=-2)[..., None]
    flux_y = jnp.maximum(wind_y[..., :, :-1, :, :], 0.0) * padded_y[..., :, :-1, :, :] + jnp.minimum(wind_y[..., :, 1:, :, :], 0.0) * padded_y[..., :, 1:, :, :]
    upper_mass = jnp.concatenate([mass_field[..., :, :, 1:, :], from_above[..., :, :, None, :]], axis=-2)
    return mass_field - (flux_x[..., 1:, :, :, :] - flux_x[..., :-1, :, :, :]) - (flux_y[..., :, 1:, :, :] - flux_y[..., :, :-1, :, :]) - fall_speed * (mass_field - upper_mass)


def face_sources(neighbours, sends, face_side):
    shift_i = (-1, 1, 0, 0)[face_side]
    shift_j = (0, 0, -1, 1)[face_side]
    opposite = (1, 0, 3, 2)[face_side]
    entry_code = neighbours[:, :, :, face_side]
    rows_i = jnp.arange(N_GX, dtype=jnp.int32)[:, None, None]
    rows_j = jnp.arange(N_GY, dtype=jnp.int32)[None, :, None]
    near_i = jnp.clip(rows_i + shift_i, 0, N_GX - 1)
    near_j = jnp.clip(rows_j + shift_j, 0, N_GY - 1)
    entry_index = jnp.clip(entry_code - SLOTS, 0, FCAP - 1)
    remote = sends[near_i, near_j, opposite, entry_index]
    is_local = entry_code < SLOTS
    source_i = jnp.where(is_local, rows_i, near_i)
    source_j = jnp.where(is_local, rows_j, near_j)
    source_s = jnp.clip(jnp.where(is_local, entry_code, remote), 0, SLOTS - 1)
    valid = (entry_code >= 0) & (is_local | (remote >= 0))
    return source_i, source_j, source_s, valid


def update_blocks(items, fall_speed, weights):
    mass_field, speed_x, speed_y = items[0], items[1], items[2]
    face_data = items[3:11]
    from_above, counts = items[11], items[12]
    advected = advect(mass_field, speed_x, speed_y, face_data[0], face_data[1], face_data[2], face_data[3], face_data[4], face_data[5], face_data[6], face_data[7], from_above, fall_speed)
    step_size = step_time / jnp.maximum(counts, 1).astype(jnp.float32)
    step_scale = step_size[..., None, None, None, None]
    for turn_index in range(SMAX):
        active = (turn_index < counts)[..., None, None, None, None]
        advected = jnp.where(active, advected + step_scale * coag_tendency(advected, weights[0], weights[1], weights[2], weights[3]), advected)
    return advected


def advance(mass_grid, wind_grid, neighbours, sends, counts, fall_speed, weights):
    speed_x = wind_grid[:, :, :, :, 0]
    speed_y = wind_grid[:, :, :, :, 1]
    layers = ((mass_grid[:, :, :, :, -1], speed_x[:, :, :, :, -1]), (mass_grid[:, :, :, :, 0], speed_x[:, :, :, :, 0]),
              (mass_grid[:, :, :, :, :, -1], speed_y[:, :, :, :, :, -1]), (mass_grid[:, :, :, :, :, 0], speed_y[:, :, :, :, :, 0]))
    levels = jnp.arange(N_GZ, dtype=jnp.int32)[None, None, :, None]
    face_data = []
    for face_side in range(4):
        source_i, source_j, source_s, valid = face_sources(neighbours, sends, face_side)
        picker = (source_i[:, :, None, :], source_j[:, :, None, :], levels, source_s[:, :, None, :])
        kept_mask = valid[:, :, None, :]
        layer_mass, layer_speed = layers[face_side]
        face_data.append(jnp.where(kept_mask[..., None, None, None], layer_mass[picker], 0.0))
        face_data.append(jnp.where(kept_mask[..., None, None], layer_speed[picker], 0.0))
    from_above = jnp.concatenate([mass_grid[:, :, 1:, :, :, :, 0], jnp.zeros_like(mass_grid[:, :, :1, :, :, :, 0])], axis=2)

    def per_column(items):
        return update_blocks(items, fall_speed, weights)

    return lax.map(per_column, (mass_grid, speed_x, speed_y) + tuple(face_data) + (from_above, counts))


def migrate(mass_grid, wind_grid, new_sources, move_lists):
    rows_i = jnp.arange(N_GX, dtype=jnp.int32)[:, None, None]
    rows_j = jnp.arange(N_GY, dtype=jnp.int32)[None, :, None]
    is_local = new_sources < SLOTS
    offset = jnp.clip(new_sources - SLOTS, 0, 3 * MCAP - 1)
    route_dir = offset // MCAP
    entry_index = offset % MCAP
    near_i = jnp.clip(rows_i + jnp.where(route_dir == 1, 0, 1), 0, N_GX - 1)
    near_j = jnp.clip(rows_j + jnp.where(route_dir == 0, 0, -1), 0, N_GY - 1)
    remote = move_lists[near_i, near_j, route_dir, entry_index]
    source_i = jnp.where(is_local, rows_i, near_i)
    source_j = jnp.where(is_local, rows_j, near_j)
    source_s = jnp.clip(jnp.where(is_local, new_sources, remote), 0, SLOTS - 1)
    levels = jnp.arange(N_GZ, dtype=jnp.int32)[None, None, :, None]
    picker = (source_i[:, :, None, :], source_j[:, :, None, :], levels, source_s[:, :, None, :])
    kept_mask = (new_sources >= 0)[:, :, None, :]
    moved_mass = jnp.where(kept_mask[..., None, None, None, None], mass_grid[picker], 0.0)
    moved_wind = jnp.where(kept_mask[..., None, None, None, None], wind_grid[picker], 0.0)
    return moved_mass, moved_wind


def reference(bin_mass, wind_field, fall_speed, gain_a, gain_b, gain_c, loss_k, old_occupied, old_neighbours, old_sends, old_substeps, move_lists, new_sources, new_neighbours, new_sends, new_substeps):
    weights = (gain_a, gain_b, gain_c, loss_k)
    mass_grid = bin_mass.reshape(N_GX, N_GY, N_GZ, SLOTS, BX, BY, BZ, BINS)
    wind_grid = wind_field.reshape(N_GX, N_GY, N_GZ, SLOTS, 2, BX, BY, BZ)
    occupied = (old_occupied > 0)[:, :, None, :]
    mass_grid = jnp.where(occupied[..., None, None, None, None], mass_grid, 0.0)
    before = old_substeps.reshape(HALF_STEPS, N_GX, N_GY, N_GZ, SLOTS)
    after = new_substeps.reshape(HALF_STEPS, N_GX, N_GY, N_GZ, SLOTS)
    for step_index in range(HALF_STEPS):
        mass_grid = advance(mass_grid, wind_grid, old_neighbours, old_sends, before[step_index], fall_speed, weights)
    mass_grid, wind_grid = migrate(mass_grid, wind_grid, new_sources, move_lists)
    for step_index in range(HALF_STEPS):
        mass_grid = advance(mass_grid, wind_grid, new_neighbours, new_sends, after[step_index], fall_speed, weights)
    return mass_grid.reshape(N_GX, N_GY, N_GZ * SLOTS, BX, BY, BZ, BINS)
```

```python
import functools

import jax
import jax.numpy as jnp
from jax import lax
from jax.experimental import pallas as pl
from jax.experimental.pallas import tpu as pltpu
from jax.sharding import PartitionSpec as P

step_time = 0.25
most_turns = 4
opposite = (1, 0, 3, 2)
MESH = pl.DeviceIdType.MESH


def split(values):
    high = values.astype(jnp.bfloat16)
    low = (values - high.astype(jnp.float32)).astype(jnp.bfloat16)
    return high, low


def kernel(
    dims,
    mass_ref,
    wind_ref,
    fall_ref,
    gain_a_ref,
    gain_b_ref,
    gain_c_ref,
    loss_k_ref,
    occupied_ref,
    old_nb_ref,
    old_sends_ref,
    old_turns_ref,
    moves_ref,
    sources_ref,
    new_nb_ref,
    new_sends_ref,
    new_turns_ref,
    out_ref,
    state,
    done,
    parcel,
    arrived,
    face_x,
    face_y,
    send_x,
    send_y,
    got_x_old,
    got_x_new,
    got_y_old,
    got_y_new,
    floor,
    got_floor_old,
    got_floor_new,
    map_one,
    map_two,
    place,
    face_out,
    face_in,
    floor_out,
    floor_in,
    move_out,
    move_in,
):
    slots, bx, by, bz, bins, fcap, mcap, peers = dims
    cells = bx * by
    entries = 3 * mcap
    got_x, got_y = (got_x_old, got_x_new), (got_y_old, got_y_new)
    got_floor = (got_floor_old, got_floor_new)
    here = tuple(lax.axis_index(name) for name in ("gx", "gy", "gz"))

    def at(shift):
        there = tuple(own + step for own, step in zip(here, shift))
        inside = True
        for spot, size in zip(there, peers):
            inside = inside & (spot >= 0) & (spot < size)
        return there, inside

    side_shift = ((-1, 0, 0), (1, 0, 0), (0, -1, 0), (0, 1, 0))
    route_shift = ((-1, 0, 0), (0, 1, 0), (-1, 1, 0))
    around = side_shift + ((0, 0, -1), (0, 0, 1), (-1, 1, 0), (1, -1, 0))

    barrier = pltpu.get_barrier_semaphore()
    for shift in around:
        there, inside = at(shift)

        @pl.when(inside)
        def _():
            pl.semaphore_signal(barrier, inc=1, device_id=there, device_id_type=MESH)

    greeted = jnp.int32(0)
    for shift in around:
        greeted = greeted + at(shift)[1].astype(jnp.int32)
    pl.semaphore_wait(barrier, greeted)

    moved = [moves_ref[0, 0, e // mcap, e % mcap] for e in range(entries)]
    count = jnp.int32(0)
    rank = []
    for entry in moved:
        rank.append(count)
        count = count + (entry >= 0).astype(jnp.int32)
    where_to = []
    for slot in range(slots):
        spot = count
        goes = jnp.int32(0)
        for entry, spot_of in zip(moved, rank):
            spot = jnp.where(entry == slot, spot_of, spot)
            goes = jnp.where(entry == slot, 1, goes)
        count = count + (1 - goes)
        where_to.append(spot)
    for slot in range(slots):
        taken = jnp.int32(0)
        for other in range(slots):
            taken = jnp.where(where_to[other] == slot, other, taken)
        place[0, slot] = taken
        place[1, slot] = where_to[slot]
    for e in range(entries):
        place[2, e] = jnp.minimum(rank[e], slots - 1)

    def speeds(wind, component, x):
        first = component * cells + x * by
        return jnp.stack(
            [jnp.broadcast_to(wind[:, first + y : first + y + 1], (bz, bins)) for y in range(by)]
        )

    def gather_faces(slot, load_x):
        wind = state[slot, cells]
        for x in range(bx):
            rows = load_x(x)
            state[slot, pl.ds(x * by, by)] = rows
            for y in range(by):
                floor[slot, x, pl.ds(y, 1), :] = rows[y, 0:1, :]
            for y, side in ((by - 1, 0), (0, 1)):
                lane = cells + x * by + y
                speed = jnp.broadcast_to(wind[:, lane : lane + 1], (bz, bins))
                bounded = jnp.maximum(speed, 0.0) if side == 0 else jnp.minimum(speed, 0.0)
                face_y[side, slot, x] = bounded * rows[y]
            if x == bx - 1:
                face_x[0, slot] = jnp.maximum(speeds(wind, 0, x), 0.0) * rows
            if x == 0:
                face_x[1, slot] = jnp.minimum(speeds(wind, 0, x), 0.0) * rows

    def exchange(turn, sends_ref):
        copies = []
        for side in range(4):
            local, out, got = (
                (face_x, send_x, got_x) if side < 2 else (face_y, send_y, got_y)
            )
            back = opposite[side]
            there, inside = at(side_shift[side])

            def pick(k, carry, side=side, local=local, out=out, back=back):
                entry = sends_ref[0, 0, side, k]
                rows = local[back % 2, jnp.clip(entry, 0, slots - 1)]
                out[turn, side % 2, k] = jnp.where(entry >= 0, rows, 0.0)
                return carry

            lax.fori_loop(0, fcap, pick, 0)
            copy = pltpu.make_async_remote_copy(
                src_ref=out.at[turn, side % 2],
                dst_ref=got[turn].at[back % 2],
                send_sem=face_out.at[turn, side],
                recv_sem=face_in.at[turn, back],
                device_id=there,
                device_id_type=MESH,
            )
            pl.when(inside)(copy.start)
            copies.append((copy, inside))
        return copies

    def send_floor(turn):
        there, inside = at((0, 0, -1))
        copy = pltpu.make_async_remote_copy(
            src_ref=floor,
            dst_ref=got_floor[turn],
            send_sem=floor_out.at[turn],
            recv_sem=floor_in.at[turn],
            device_id=there,
            device_id_type=MESH,
        )
        pl.when(inside)(copy.start)
        return copy, inside

    def await_faces(turn, floor_copy):
        copy, _ = floor_copy
        _, above_inside = at((0, 0, 1))
        for side in range(4):
            _, inside = at(side_shift[side])
            got = got_x if side < 2 else got_y
            landing = pltpu.make_async_remote_copy(
                src_ref=got[turn].at[side % 2],
                dst_ref=got[turn].at[side % 2],
                send_sem=face_out.at[turn, side],
                recv_sem=face_in.at[turn, side],
                device_id=at(side_shift[side])[0],
                device_id_type=MESH,
            )
            pl.when(inside)(landing.wait_recv)
        pl.when(above_inside)(copy.wait_recv)

    def await_sent(copies, floor_copy):
        for copy, inside in copies + [floor_copy]:
            pl.when(inside)(copy.wait_send)

    def step(turn, slot, nb_ref, turns_ref, target, spot):
        wind = state[slot, cells]
        ghosts = []
        for side in range(4):
            local, got = (face_x, got_x) if side < 2 else (face_y, got_y)
            code = nb_ref[0, 0, slot, side]
            near = local[side % 2, jnp.clip(code, 0, slots - 1)]
            far = got[turn][side % 2, jnp.clip(code - slots, 0, fcap - 1)]
            ghosts.append(jnp.where(code < 0, 0.0, jnp.where(code < slots, near, far)))
        west, east, south, north = ghosts
        has_above = here[2] + 1 < peers[2]
        fall = fall_ref[...].reshape(1, 1, bins)
        level = lax.broadcasted_iota(jnp.int32, (by, bz, bins), 1)
        rows = state[slot, pl.ds(0, by)]
        speed = speeds(wind, 0, 0)
        behind = west
        for x in range(bx):
            upward = jnp.maximum(speed, 0.0) * rows
            downward = jnp.minimum(speed, 0.0) * rows
            if x + 1 < bx:
                later = state[slot, pl.ds((x + 1) * by, by)]
                later_speed = speeds(wind, 0, x + 1)
                ahead = jnp.minimum(later_speed, 0.0) * later
            else:
                ahead = east
            total_x = (upward + ahead) - (behind + downward)
            speed_y = speeds(wind, 1, x)
            up_y = jnp.maximum(speed_y, 0.0) * rows
            down_y = jnp.minimum(speed_y, 0.0) * rows
            ahead_y = jnp.concatenate([down_y[1:], north[x][None]], axis=0)
            behind_y = jnp.concatenate([south[x][None], up_y[:-1]], axis=0)
            total_y = (up_y + ahead_y) - (behind_y + down_y)
            top = jnp.stack(
                [
                    jnp.broadcast_to(got_floor[turn][slot, x, pl.ds(y, 1), :], (bz, bins))
                    for y in range(by)
                ]
            )
            top = jnp.where(has_above, top, 0.0)
            upper = jnp.where(level == bz - 1, top, pltpu.roll(rows, bz - 1, 1))
            target[spot, pl.ds(x * by, by)] = rows - total_x - total_y - fall * (rows - upper)
            behind = upward
            if x + 1 < bx:
                rows, speed = later, later_speed
        turns = turns_ref[0, 0, 0, slot]
        size = step_time / jnp.maximum(jnp.full((1, bins), turns, jnp.int32), 1).astype(jnp.float32)

        def coagulate(index, carry):
            mass = target[spot, pl.ds(0, cells)].reshape(cells * bz, bins)
            high, low = split(mass)
            first = jnp.dot(
                jnp.concatenate([high, low], axis=1),
                map_one[...],
                preferred_element_type=jnp.float32,
            )
            parts = [first[:, i * bins : (i + 1) * bins] for i in range(6)]
            paired = (parts[0] + parts[3]) * (parts[1] + parts[4])
            lost = mass * (parts[2] + parts[5])
            high, low = split(paired)
            second = jnp.dot(
                jnp.concatenate([high, low], axis=1),
                map_two[...],
                preferred_element_type=jnp.float32,
            )
            gained = second[:, :bins] + second[:, bins:]
            changed = jnp.where(index < turns, mass + size * (gained - lost), mass)
            target[spot, pl.ds(0, cells)] = changed.reshape(cells, bz, bins)
            return carry

        lax.fori_loop(0, most_turns, coagulate, 0)

    def first_faces(slot, carry):
        held = occupied_ref[0, 0, slot] > 0
        state[slot, cells] = wind_ref[slot]
        gather_faces(
            slot, lambda x: jnp.where(held, mass_ref[slot, pl.ds(x * by, by)], 0.0)
        )
        return carry

    lax.fori_loop(0, slots, first_faces, 0)
    copies = exchange(0, old_sends_ref)
    floor_copy = send_floor(0)
    for i, ref in enumerate((gain_a_ref, gain_b_ref, loss_k_ref)):
        for row in (0, bins):
            for part, values in enumerate(split(ref[...])):
                map_one[pl.ds(row, bins), pl.ds((part * 3 + i) * bins, bins)] = values
    for row in (0, bins):
        for part, values in enumerate(split(gain_c_ref[...])):
            map_two[pl.ds(row, bins), pl.ds(part * bins, bins)] = values
    await_faces(0, floor_copy)

    def move_copy(e):
        route = e // mcap
        west_leg = jnp.where(route == 1, 0, -1)
        north_leg = jnp.where(route == 0, 0, 1)
        there, inside = at((west_leg, north_leg, 0))
        _, incoming = at((-west_leg, -north_leg, 0))
        copy = pltpu.make_async_remote_copy(
            src_ref=parcel.at[e],
            dst_ref=arrived.at[e],
            send_sem=move_out.at[e],
            recv_sem=move_in.at[e],
            device_id=there,
            device_id_type=MESH,
        )
        return copy, inside, incoming

    def post(e, carry):
        copy, inside, _ = move_copy(e)
        parcel[e] = done[place[2, e]]
        pl.when(inside)(copy.start)
        return carry

    def first_step(spot, carry):
        slot = place[0, spot]
        step(0, slot, old_nb_ref, old_turns_ref, done, spot)
        done[spot, cells] = state[slot, cells]
        return carry

    def first_and_post(spot, carry):
        first_step(spot, carry)
        return post(spot, carry)

    shared = min(slots, entries)
    lax.fori_loop(0, shared, first_and_post, 0)
    if slots > shared:
        lax.fori_loop(shared, slots, first_step, 0)
    if entries > shared:
        lax.fori_loop(shared, entries, post, 0)
    await_sent(copies, floor_copy)

    def land(e, carry):
        copy, _, incoming = move_copy(e)
        pl.when(incoming)(copy.wait_recv)
        return carry

    lax.fori_loop(0, entries, land, 0)

    def second_faces(slot, carry):
        code = sources_ref[0, 0, slot]
        own = place[1, jnp.clip(code, 0, slots - 1)]
        came = jnp.clip(code - slots, 0, entries - 1)

        def choose(first, length):
            near = done[own, pl.ds(first, length)]
            far = arrived[came, pl.ds(first, length)]
            return jnp.where(code < 0, 0.0, jnp.where(code < slots, near, far))

        state[slot, cells] = choose(cells, 1)[0]
        gather_faces(slot, lambda x: choose(x * by, by))
        return carry

    lax.fori_loop(0, slots, second_faces, 0)
    copies = exchange(1, new_sends_ref)
    floor_copy = send_floor(1)
    await_faces(1, floor_copy)

    def second_step(slot, carry):
        step(1, slot, new_nb_ref, new_turns_ref, out_ref, slot)
        return carry

    lax.fori_loop(0, slots, second_step, 0)
    await_sent(copies, floor_copy)

    def sent(e, carry):
        copy, inside, _ = move_copy(e)
        pl.when(inside)(copy.wait_send)
        return carry

    lax.fori_loop(0, entries, sent, 0)


def on_device(peers, bin_mass, wind_field, fall_speed, *rest):
    slots, bx, by, bz, bins = bin_mass.shape[2:]
    cells = bx * by
    old_sends, move_lists = rest[6], rest[8]
    fcap, mcap = old_sends.shape[-1], move_lists.shape[-1]
    entries = 3 * mcap
    wind = wind_field.reshape(slots, 2 * bx * by, bz).transpose(0, 2, 1)
    dims = (slots, bx, by, bz, bins, fcap, mcap, peers)
    vmem = pl.BlockSpec(memory_space=pltpu.VMEM)
    smem = pl.BlockSpec(memory_space=pltpu.SMEM)
    f32 = jnp.float32
    result = pl.pallas_call(
        functools.partial(kernel, dims),
        out_shape=jax.ShapeDtypeStruct((slots, cells, bz, bins), f32),
        in_specs=[vmem] * 7 + [smem] * 9,
        out_specs=vmem,
        scratch_shapes=[
            pltpu.VMEM((slots, cells + 1, bz, bins), f32),
            pltpu.VMEM((slots, cells + 1, bz, bins), f32),
            pltpu.VMEM((entries, cells + 1, bz, bins), f32),
            pltpu.VMEM((entries, cells + 1, bz, bins), f32),
            pltpu.VMEM((2, slots, by, bz, bins), f32),
            pltpu.VMEM((2, slots, bx, bz, bins), f32),
            pltpu.VMEM((2, 2, fcap, by, bz, bins), f32),
            pltpu.VMEM((2, 2, fcap, bx, bz, bins), f32),
            pltpu.VMEM((2, fcap, by, bz, bins), f32),
            pltpu.VMEM((2, fcap, by, bz, bins), f32),
            pltpu.VMEM((2, fcap, bx, bz, bins), f32),
            pltpu.VMEM((2, fcap, bx, bz, bins), f32),
            pltpu.VMEM((slots, bx, by, bins), f32),
            pltpu.VMEM((slots, bx, by, bins), f32),
            pltpu.VMEM((slots, bx, by, bins), f32),
            pltpu.VMEM((2 * bins, 6 * bins), jnp.bfloat16),
            pltpu.VMEM((2 * bins, 2 * bins), jnp.bfloat16),
            pltpu.SMEM((3, max(slots, entries)), jnp.int32),
            pltpu.SemaphoreType.DMA((2, 4)),
            pltpu.SemaphoreType.DMA((2, 4)),
            pltpu.SemaphoreType.DMA((2,)),
            pltpu.SemaphoreType.DMA((2,)),
            pltpu.SemaphoreType.DMA((entries,)),
            pltpu.SemaphoreType.DMA((entries,)),
        ],
        compiler_params=pltpu.CompilerParams(
            collective_id=0, has_side_effects=True, vmem_limit_bytes=40 * 1024 * 1024
        ),
    )(
        bin_mass.reshape(slots, cells, bz, bins),
        wind,
        fall_speed.reshape(1, bins),
        *rest,
    )
    return result.reshape(bin_mass.shape)


def solution(mesh):
    peers = tuple(mesh.shape[name] for name in ("gx", "gy", "gz"))
    placed = (
        P("gx", "gy", "gz", None, None, None, None),
        P("gx", "gy", "gz", None, None, None),
        P(),
        P(),
        P(),
        P(),
        P(),
        P("gx", "gy", None),
        P("gx", "gy", None, None),
        P("gx", "gy", None, None),
        P(None, "gx", "gy", "gz"),
        P("gx", "gy", None, None),
        P("gx", "gy", None),
        P("gx", "gy", None, None),
        P("gx", "gy", None, None),
        P(None, "gx", "gy", "gz"),
    )
    return jax.shard_map(
        functools.partial(on_device, peers),
        mesh=mesh,
        in_specs=placed,
        out_specs=P("gx", "gy", "gz", None, None, None, None),
        check_vma=False,
    )
```

```python
import functools

import jax
import jax.numpy as jnp
from jax import lax
from jax.experimental import pallas as pl
from jax.experimental.pallas import tpu as pltpu
from jax.sharding import PartitionSpec as P

step_time = 0.25
most_turns = 4
opposite = (1, 0, 3, 2)
MESH = pl.DeviceIdType.MESH


def split(values):
    high = values.astype(jnp.bfloat16)
    low = (values - high.astype(jnp.float32)).astype(jnp.bfloat16)
    return high, low


def kernel(dims, *refs):
    far_mass, far_small, out_ref = refs[0], refs[1:16], refs[16]
    mass_ref, small_refs, (fetched_mass, fetched_small) = refs[17], refs[18:33], refs[33:35]
    wind_ref, fall_ref, gain_a_ref, gain_b_ref, gain_c_ref, loss_k_ref = small_refs[:6]
    occupied_ref, old_nb_ref, old_sends_ref, old_turns_ref, moves_ref = small_refs[6:11]
    sources_ref, new_nb_ref, new_sends_ref, new_turns_ref = small_refs[11:]
    state, done, parcel, arrived, face_x, face_y, send_x, send_y = refs[35:43]
    got_x_old, got_x_new, got_y_old, got_y_new, floor = refs[43:48]
    got_floor_old, got_floor_new, map_one, map_two, place = refs[48:53]
    face_out, face_in, floor_out, floor_in, move_out, move_in = refs[53:]
    slots, bx, by, bz, bins, fcap, mcap, peers = dims
    cells = bx * by
    entries = 3 * mcap
    got_x, got_y = (got_x_old, got_x_new), (got_y_old, got_y_new)
    got_floor = (got_floor_old, got_floor_new)
    here = tuple(lax.axis_index(name) for name in ("gx", "gy", "gz"))

    def at(shift):
        there = tuple(own + step for own, step in zip(here, shift))
        inside = True
        for spot, size in zip(there, peers):
            inside = inside & (spot >= 0) & (spot < size)
        return there, inside

    side_shift = ((-1, 0, 0), (1, 0, 0), (0, -1, 0), (0, 1, 0))
    route_shift = ((-1, 0, 0), (0, 1, 0), (-1, 1, 0))
    around = side_shift + ((0, 0, -1), (0, 0, 1), (-1, 1, 0), (1, -1, 0))

    def fetch_mass(slot):
        return pltpu.make_async_copy(
            far_mass.at[slot], mass_ref.at[slot], fetched_mass.at[slot]
        )

    fetches = [
        pltpu.make_async_copy(far, near, fetched_small.at[i])
        for i, (far, near) in enumerate(zip(far_small, small_refs))
    ]
    for fetch in fetches[6:] + fetches[:1]:
        fetch.start()
    for slot in range(slots):
        fetch_mass(slot).start()
    for fetch in fetches[1:6]:
        fetch.start()

    barrier = pltpu.get_barrier_semaphore()
    for shift in around:
        there, inside = at(shift)

        @pl.when(inside)
        def _():
            pl.semaphore_signal(barrier, inc=1, device_id=there, device_id_type=MESH)

    greeted = jnp.int32(0)
    for shift in around:
        greeted = greeted + at(shift)[1].astype(jnp.int32)
    pl.semaphore_wait(barrier, greeted)

    for fetch in fetches[6:] + fetches[:1]:
        fetch.wait()

    moved = [moves_ref[0, 0, e % mcap, e // mcap] for e in range(entries)]
    count = jnp.int32(0)
    rank = []
    for entry in moved:
        rank.append(count)
        count = count + (entry >= 0).astype(jnp.int32)
    where_to = []
    for slot in range(slots):
        spot = count
        goes = jnp.int32(0)
        for entry, spot_of in zip(moved, rank):
            spot = jnp.where(entry == slot, spot_of, spot)
            goes = jnp.where(entry == slot, 1, goes)
        count = count + (1 - goes)
        where_to.append(spot)
    for slot in range(slots):
        taken = jnp.int32(0)
        for other in range(slots):
            taken = jnp.where(where_to[other] == slot, other, taken)
        place[0, slot] = taken
        place[1, slot] = where_to[slot]
    for e in range(entries):
        place[2, e] = jnp.minimum(rank[e], slots - 1)

    def speeds(wind, component, x):
        return jnp.stack([speed_at(wind, component, x, y) for y in range(by)])

    def speed_at(wind, component, x, y):
        lane = (y * 2 + component) * bx + x
        return jnp.broadcast_to(wind[:, lane : lane + 1], (bz, bins))

    def gather_faces(slot, load_x):
        wind = state[slot, cells]
        for x in range(bx):
            rows = load_x(x)
            state[slot, pl.ds(x * by, by)] = rows
            for y in range(by):
                floor[slot, x, pl.ds(y, 1), :] = rows[y, 0:1, :]
            for y, side in ((by - 1, 0), (0, 1)):
                speed = speed_at(wind, 1, x, y)
                bounded = jnp.maximum(speed, 0.0) if side == 0 else jnp.minimum(speed, 0.0)
                face_y[side, slot, x] = bounded * rows[y]
            if x == bx - 1:
                face_x[0, slot] = jnp.maximum(speeds(wind, 0, x), 0.0) * rows
            if x == 0:
                face_x[1, slot] = jnp.minimum(speeds(wind, 0, x), 0.0) * rows

    def exchange(turn, sends_ref):
        copies = []
        for side in range(4):
            local, out, got = (
                (face_x, send_x, got_x) if side < 2 else (face_y, send_y, got_y)
            )
            back = opposite[side]
            there, inside = at(side_shift[side])

            def pick(k, carry, side=side, local=local, out=out, back=back):
                entry = sends_ref[0, k, 0, side]
                rows = local[back % 2, jnp.clip(entry, 0, slots - 1)]
                out[turn, side % 2, k] = jnp.where(entry >= 0, rows, 0.0)
                return carry

            lax.fori_loop(0, fcap, pick, 0)
            copy = pltpu.make_async_remote_copy(
                src_ref=out.at[turn, side % 2],
                dst_ref=got[turn].at[back % 2],
                send_sem=face_out.at[turn, side],
                recv_sem=face_in.at[turn, back],
                device_id=there,
                device_id_type=MESH,
            )
            pl.when(inside)(copy.start)
            copies.append((copy, inside))
        return copies

    def send_floor(turn):
        there, inside = at((0, 0, -1))
        copy = pltpu.make_async_remote_copy(
            src_ref=floor,
            dst_ref=got_floor[turn],
            send_sem=floor_out.at[turn],
            recv_sem=floor_in.at[turn],
            device_id=there,
            device_id_type=MESH,
        )
        pl.when(inside)(copy.start)
        return copy, inside

    def await_faces(turn, floor_copy):
        copy, _ = floor_copy
        _, above_inside = at((0, 0, 1))
        for side in range(4):
            _, inside = at(side_shift[side])
            got = got_x if side < 2 else got_y
            landing = pltpu.make_async_remote_copy(
                src_ref=got[turn].at[side % 2],
                dst_ref=got[turn].at[side % 2],
                send_sem=face_out.at[turn, side],
                recv_sem=face_in.at[turn, side],
                device_id=at(side_shift[side])[0],
                device_id_type=MESH,
            )
            pl.when(inside)(landing.wait_recv)
        pl.when(above_inside)(copy.wait_recv)

    def await_sent(copies, floor_copy):
        for copy, inside in copies + [floor_copy]:
            pl.when(inside)(copy.wait_send)

    def step(turn, slot, nb_ref, turns_ref, target, spot):
        wind = state[slot, cells]
        ghosts = []
        for side in range(4):
            local, got = (face_x, got_x) if side < 2 else (face_y, got_y)
            code = nb_ref[0, 0, side, slot]
            near = local[side % 2, jnp.clip(code, 0, slots - 1)]
            far = got[turn][side % 2, jnp.clip(code - slots, 0, fcap - 1)]
            ghosts.append(jnp.where(code < 0, 0.0, jnp.where(code < slots, near, far)))
        west, east, south, north = ghosts
        has_above = here[2] + 1 < peers[2]
        fall = fall_ref[...].reshape(1, 1, bins)
        level = lax.broadcasted_iota(jnp.int32, (by, bz, bins), 1)
        rows = state[slot, pl.ds(0, by)]
        speed = speeds(wind, 0, 0)
        behind = west
        for x in range(bx):
            upward = jnp.maximum(speed, 0.0) * rows
            downward = jnp.minimum(speed, 0.0) * rows
            if x + 1 < bx:
                later = state[slot, pl.ds((x + 1) * by, by)]
                later_speed = speeds(wind, 0, x + 1)
                ahead = jnp.minimum(later_speed, 0.0) * later
            else:
                ahead = east
            total_x = (upward + ahead) - (behind + downward)
            speed_y = speeds(wind, 1, x)
            up_y = jnp.maximum(speed_y, 0.0) * rows
            down_y = jnp.minimum(speed_y, 0.0) * rows
            ahead_y = jnp.concatenate([down_y[1:], north[x][None]], axis=0)
            behind_y = jnp.concatenate([south[x][None], up_y[:-1]], axis=0)
            total_y = (up_y + ahead_y) - (behind_y + down_y)
            top = jnp.stack(
                [
                    jnp.broadcast_to(got_floor[turn][slot, x, pl.ds(y, 1), :], (bz, bins))
                    for y in range(by)
                ]
            )
            top = jnp.where(has_above, top, 0.0)
            upper = jnp.where(level == bz - 1, top, pltpu.roll(rows, bz - 1, 1))
            target[spot, pl.ds(x * by, by)] = rows - total_x - total_y - fall * (rows - upper)
            behind = upward
            if x + 1 < bx:
                rows, speed = later, later_speed
        turns = turns_ref[0, 0, 0, slot]
        size = step_time / jnp.maximum(jnp.full((1, bins), turns, jnp.int32), 1).astype(jnp.float32)

        def coagulate(index, carry):
            mass = target[spot, pl.ds(0, cells)].reshape(cells * bz, bins)
            high, low = split(mass)
            first = jnp.dot(
                jnp.concatenate([high, low], axis=1),
                map_one[...],
                preferred_element_type=jnp.float32,
            )
            parts = [first[:, i * bins : (i + 1) * bins] for i in range(6)]
            paired = (parts[0] + parts[3]) * (parts[1] + parts[4])
            lost = mass * (parts[2] + parts[5])
            high, low = split(paired)
            second = jnp.dot(
                jnp.concatenate([high, low], axis=1),
                map_two[...],
                preferred_element_type=jnp.float32,
            )
            gained = second[:, :bins] + second[:, bins:]
            changed = jnp.where(index < turns, mass + size * (gained - lost), mass)
            target[spot, pl.ds(0, cells)] = changed.reshape(cells, bz, bins)
            return carry

        lax.fori_loop(0, most_turns, coagulate, 0)

    def first_faces(slot, carry):
        fetch_mass(slot).wait()
        held = occupied_ref[0, 0, slot] > 0
        columns = wind_ref[0, 0, slot].reshape(2 * bx, by * bz).T
        for y in range(by):
            state[slot, cells, :, pl.ds(y * 2 * bx, 2 * bx)] = columns[y * bz : (y + 1) * bz]
        gather_faces(
            slot, lambda x: jnp.where(held, mass_ref[slot, pl.ds(x * by, by)], 0.0)
        )
        return carry

    lax.fori_loop(0, slots, first_faces, 0)
    copies = exchange(0, old_sends_ref)
    floor_copy = send_floor(0)
    for fetch in fetches[1:6]:
        fetch.wait()
    for i, ref in enumerate((gain_a_ref, gain_b_ref, loss_k_ref)):
        for row in (0, bins):
            for part, values in enumerate(split(ref[...])):
                map_one[pl.ds(row, bins), pl.ds((part * 3 + i) * bins, bins)] = values
    for row in (0, bins):
        for part, values in enumerate(split(gain_c_ref[...])):
            map_two[pl.ds(row, bins), pl.ds(part * bins, bins)] = values
    await_faces(0, floor_copy)

    def move_copy(e):
        route = e // mcap
        west_leg = jnp.where(route == 1, 0, -1)
        north_leg = jnp.where(route == 0, 0, 1)
        there, inside = at((west_leg, north_leg, 0))
        _, incoming = at((-west_leg, -north_leg, 0))
        copy = pltpu.make_async_remote_copy(
            src_ref=parcel.at[e],
            dst_ref=arrived.at[e],
            send_sem=move_out.at[e],
            recv_sem=move_in.at[e],
            device_id=there,
            device_id_type=MESH,
        )
        return copy, inside, incoming

    def post(e, carry):
        copy, inside, _ = move_copy(e)
        parcel[e] = done[place[2, e]]
        pl.when(inside)(copy.start)
        return carry

    def first_step(spot, carry):
        slot = place[0, spot]
        step(0, slot, old_nb_ref, old_turns_ref, done, spot)
        done[spot, cells] = state[slot, cells]
        return carry

    def first_and_post(spot, carry):
        first_step(spot, carry)
        return post(spot, carry)

    shared = min(slots, entries)
    lax.fori_loop(0, shared, first_and_post, 0)
    if slots > shared:
        lax.fori_loop(shared, slots, first_step, 0)
    if entries > shared:
        lax.fori_loop(shared, entries, post, 0)
    await_sent(copies, floor_copy)

    def land(e, carry):
        copy, _, incoming = move_copy(e)
        pl.when(incoming)(copy.wait_recv)
        return carry

    lax.fori_loop(0, entries, land, 0)

    def second_faces(slot, carry):
        code = sources_ref[0, 0, slot]
        own = place[1, jnp.clip(code, 0, slots - 1)]
        came = jnp.clip(code - slots, 0, entries - 1)

        def choose(first, length):
            near = done[own, pl.ds(first, length)]
            far = arrived[came, pl.ds(first, length)]
            return jnp.where(code < 0, 0.0, jnp.where(code < slots, near, far))

        state[slot, cells] = choose(cells, 1)[0]
        gather_faces(slot, lambda x: choose(x * by, by))
        return carry

    lax.fori_loop(0, slots, second_faces, 0)
    copies = exchange(1, new_sends_ref)
    floor_copy = send_floor(1)
    await_faces(1, floor_copy)

    def second_step(slot, carry):
        step(1, slot, new_nb_ref, new_turns_ref, out_ref, slot)
        return carry

    lax.fori_loop(0, slots, second_step, 0)
    await_sent(copies, floor_copy)

    def sent(e, carry):
        copy, inside, _ = move_copy(e)
        pl.when(inside)(copy.wait_send)
        return carry

    lax.fori_loop(0, entries, sent, 0)


def on_device(peers, bin_mass, wind_field, fall_speed, *rest):
    slots, bx, by, bz, bins = bin_mass.shape[2:]
    cells = bx * by
    old_sends, move_lists = rest[6], rest[8]
    fcap, mcap = old_sends.shape[-1], move_lists.shape[-1]
    entries = 3 * mcap
    small = [wind_field, fall_speed.reshape(1, bins), *rest]
    for i in (7, 12):
        small[i] = small[i].transpose(0, 1, 3, 2)
    for i in (8, 13):
        small[i] = small[i].transpose(0, 3, 1, 2)
    small[10] = small[10].transpose(0, 1, 3, 2)
    dims = (slots, bx, by, bz, bins, fcap, mcap, peers)
    vmem = pl.BlockSpec(memory_space=pltpu.VMEM)
    hbm = pl.BlockSpec(memory_space=pltpu.HBM)
    f32 = jnp.float32
    result = pl.pallas_call(
        functools.partial(kernel, dims),
        out_shape=jax.ShapeDtypeStruct((slots, cells, bz, bins), f32),
        in_specs=[hbm] * 16,
        out_specs=vmem,
        scratch_shapes=[
            pltpu.VMEM((slots, cells, bz, bins), f32),
            *[pltpu.VMEM(array.shape, f32) for array in small[:6]],
            *[pltpu.SMEM(array.shape, jnp.int32) for array in small[6:]],
            pltpu.SemaphoreType.DMA((slots,)),
            pltpu.SemaphoreType.DMA((len(small),)),
            pltpu.VMEM((slots, cells + 1, bz, bins), f32),
            pltpu.VMEM((slots, cells + 1, bz, bins), f32),
            pltpu.VMEM((entries, cells + 1, bz, bins), f32),
            pltpu.VMEM((entries, cells + 1, bz, bins), f32),
            pltpu.VMEM((2, slots, by, bz, bins), f32),
            pltpu.VMEM((2, slots, bx, bz, bins), f32),
            pltpu.VMEM((2, 2, fcap, by, bz, bins), f32),
            pltpu.VMEM((2, 2, fcap, bx, bz, bins), f32),
            pltpu.VMEM((2, fcap, by, bz, bins), f32),
            pltpu.VMEM((2, fcap, by, bz, bins), f32),
            pltpu.VMEM((2, fcap, bx, bz, bins), f32),
            pltpu.VMEM((2, fcap, bx, bz, bins), f32),
            pltpu.VMEM((slots, bx, by, bins), f32),
            pltpu.VMEM((slots, bx, by, bins), f32),
            pltpu.VMEM((slots, bx, by, bins), f32),
            pltpu.VMEM((2 * bins, 6 * bins), jnp.bfloat16),
            pltpu.VMEM((2 * bins, 2 * bins), jnp.bfloat16),
            pltpu.SMEM((3, max(slots, entries)), jnp.int32),
            pltpu.SemaphoreType.DMA((2, 4)),
            pltpu.SemaphoreType.DMA((2, 4)),
            pltpu.SemaphoreType.DMA((2,)),
            pltpu.SemaphoreType.DMA((2,)),
            pltpu.SemaphoreType.DMA((entries,)),
            pltpu.SemaphoreType.DMA((entries,)),
        ],
        compiler_params=pltpu.CompilerParams(
            collective_id=0, has_side_effects=True, vmem_limit_bytes=56 * 1024 * 1024
        ),
    )(
        bin_mass.reshape(slots, cells, bz, bins),
        *small,
    )
    return result.reshape(bin_mass.shape)


def solution(mesh):
    peers = tuple(mesh.shape[name] for name in ("gx", "gy", "gz"))
    placed = (
        P("gx", "gy", "gz", None, None, None, None),
        P("gx", "gy", "gz", None, None, None),
        P(),
        P(),
        P(),
        P(),
        P(),
        P("gx", "gy", None),
        P("gx", "gy", None, None),
        P("gx", "gy", None, None),
        P(None, "gx", "gy", "gz"),
        P("gx", "gy", None, None),
        P("gx", "gy", None),
        P("gx", "gy", None, None),
        P("gx", "gy", None, None),
        P(None, "gx", "gy", "gz"),
    )
    return jax.shard_map(
        functools.partial(on_device, peers),
        mesh=mesh,
        in_specs=placed,
        out_specs=P("gx", "gy", "gz", None, None, None, None),
        check_vma=False,
    )
```

```python
import functools

import jax
import jax.numpy as jnp
from jax import lax
from jax.experimental import pallas as pl
from jax.experimental.pallas import tpu as pltpu
from jax.sharding import PartitionSpec as P

step_time = 0.25
most_turns = 4
opposite = (1, 0, 3, 2)
MESH = pl.DeviceIdType.MESH


def split(values):
    high = values.astype(jnp.bfloat16)
    low = (values - high.astype(jnp.float32)).astype(jnp.bfloat16)
    return high, low


def product(rows, map_ref):
    return jnp.dot(
        jnp.concatenate(split(rows), axis=1), map_ref[...], preferred_element_type=jnp.float32
    )


def kernel(dims, *refs):
    far_mass, far_small, out_ref = refs[0], refs[1:16], refs[16]
    mass_ref, small_refs, (fetched_mass, fetched_small) = refs[17], refs[18:33], refs[33:35]
    wind_ref, fall_ref, gain_a_ref, gain_b_ref, gain_c_ref, loss_k_ref = small_refs[:6]
    occupied_ref, old_nb_ref, old_sends_ref, old_turns_ref, moves_ref = small_refs[6:11]
    sources_ref, new_nb_ref, new_sends_ref, new_turns_ref = small_refs[11:]
    state, done, parcel, arrived, face_x, face_y, send_x, send_y = refs[35:43]
    got_x_old, got_x_new, got_y_old, got_y_new, floor = refs[43:48]
    got_floor_old, got_floor_new, map_one, map_two, place = refs[48:53]
    face_out, face_in, floor_out, floor_in, move_out, move_in = refs[53:]
    slots, bx, by, bz, bins, fcap, mcap, peers = dims
    cells = bx * by
    entries = 3 * mcap
    got_x, got_y = (got_x_old, got_x_new), (got_y_old, got_y_new)
    got_floor = (got_floor_old, got_floor_new)
    here = tuple(lax.axis_index(name) for name in ("gx", "gy", "gz"))

    def at(shift):
        there = tuple(own + step for own, step in zip(here, shift))
        inside = True
        for spot, size in zip(there, peers):
            inside = inside & (spot >= 0) & (spot < size)
        return there, inside

    side_shift = ((-1, 0, 0), (1, 0, 0), (0, -1, 0), (0, 1, 0))
    route_shift = ((-1, 0, 0), (0, 1, 0), (-1, 1, 0))
    around = side_shift + ((0, 0, -1), (0, 0, 1), (-1, 1, 0), (1, -1, 0))

    def fetch_mass(slot):
        return pltpu.make_async_copy(
            far_mass.at[slot], mass_ref.at[slot], fetched_mass.at[slot]
        )

    fetches = [
        pltpu.make_async_copy(far, near, fetched_small.at[i])
        for i, (far, near) in enumerate(zip(far_small, small_refs))
    ]
    for fetch in fetches[6:] + fetches[:1]:
        fetch.start()
    for slot in range(slots):
        fetch_mass(slot).start()
    for fetch in fetches[1:6]:
        fetch.start()

    barrier = pltpu.get_barrier_semaphore()
    for shift in around:
        there, inside = at(shift)

        @pl.when(inside)
        def _():
            pl.semaphore_signal(barrier, inc=1, device_id=there, device_id_type=MESH)

    greeted = jnp.int32(0)
    for shift in around:
        greeted = greeted + at(shift)[1].astype(jnp.int32)
    pl.semaphore_wait(barrier, greeted)

    for fetch in fetches[6:] + fetches[:1]:
        fetch.wait()

    moved = [moves_ref[0, 0, e % mcap, e // mcap] for e in range(entries)]
    count = jnp.int32(0)
    rank = []
    for entry in moved:
        rank.append(count)
        count = count + (entry >= 0).astype(jnp.int32)
    where_to = []
    for slot in range(slots):
        spot = count
        goes = jnp.int32(0)
        for entry, spot_of in zip(moved, rank):
            spot = jnp.where(entry == slot, spot_of, spot)
            goes = jnp.where(entry == slot, 1, goes)
        count = count + (1 - goes)
        where_to.append(spot)
    for slot in range(slots):
        taken = jnp.int32(0)
        for other in range(slots):
            taken = jnp.where(where_to[other] == slot, other, taken)
        place[0, slot] = taken
        place[1, slot] = where_to[slot]
    for e in range(entries):
        place[2, e] = jnp.minimum(rank[e], slots - 1)

    def speeds(wind, component, x):
        return jnp.stack([speed_at(wind, component, x, y) for y in range(by)])

    def speed_at(wind, component, x, y):
        lane = (y * 2 + component) * bx + x
        return jnp.broadcast_to(wind[:, lane : lane + 1], (bz, bins))

    def gather_faces(slot, load_x):
        wind = state[slot, cells]
        for x in range(bx):
            rows = load_x(x)
            state[slot, pl.ds(x * by, by)] = rows
            for y in range(by):
                floor[slot, x, pl.ds(y, 1), :] = rows[y, 0:1, :]
            for y, side in ((by - 1, 0), (0, 1)):
                speed = speed_at(wind, 1, x, y)
                bounded = jnp.maximum(speed, 0.0) if side == 0 else jnp.minimum(speed, 0.0)
                face_y[side, slot, x] = bounded * rows[y]
            if x == bx - 1:
                face_x[0, slot] = jnp.maximum(speeds(wind, 0, x), 0.0) * rows
            if x == 0:
                face_x[1, slot] = jnp.minimum(speeds(wind, 0, x), 0.0) * rows

    def exchange(turn, sends_ref):
        copies = []
        for side in range(4):
            local, out, got = (
                (face_x, send_x, got_x) if side < 2 else (face_y, send_y, got_y)
            )
            back = opposite[side]
            there, inside = at(side_shift[side])

            def pick(k, carry, side=side, local=local, out=out, back=back):
                entry = sends_ref[0, k, 0, side]
                rows = local[back % 2, jnp.clip(entry, 0, slots - 1)]
                out[turn, side % 2, k] = jnp.where(entry >= 0, rows, 0.0)
                return carry

            lax.fori_loop(0, fcap, pick, 0)
            copy = pltpu.make_async_remote_copy(
                src_ref=out.at[turn, side % 2],
                dst_ref=got[turn].at[back % 2],
                send_sem=face_out.at[turn, side],
                recv_sem=face_in.at[turn, back],
                device_id=there,
                device_id_type=MESH,
            )
            pl.when(inside)(copy.start)
            copies.append((copy, inside))
        return copies

    def floor_copy(turn, slot):
        return pltpu.make_async_remote_copy(
            src_ref=floor.at[slot],
            dst_ref=got_floor[turn].at[slot],
            send_sem=floor_out.at[turn, slot],
            recv_sem=floor_in.at[turn, slot],
            device_id=at((0, 0, -1))[0],
            device_id_type=MESH,
        )

    def send_floor(turn, slot):
        pl.when(at((0, 0, -1))[1])(floor_copy(turn, slot).start)

    def await_faces(turn):
        _, above_inside = at((0, 0, 1))
        for side in range(4):
            _, inside = at(side_shift[side])
            got = got_x if side < 2 else got_y
            landing = pltpu.make_async_remote_copy(
                src_ref=got[turn].at[side % 2],
                dst_ref=got[turn].at[side % 2],
                send_sem=face_out.at[turn, side],
                recv_sem=face_in.at[turn, side],
                device_id=at(side_shift[side])[0],
                device_id_type=MESH,
            )
            pl.when(inside)(landing.wait_recv)

        @pl.when(above_inside)
        def _():
            for slot in range(slots):
                floor_copy(turn, slot).wait_recv()

    def await_sent(turn, copies):
        for copy, inside in copies:
            pl.when(inside)(copy.wait_send)

        @pl.when(at((0, 0, -1))[1])
        def _():
            for slot in range(slots):
                floor_copy(turn, slot).wait_send()

    def step(turn, slot, nb_ref, turns_ref, target, spot):
        wind = state[slot, cells]
        ghosts = []
        for side in range(4):
            local, got = (face_x, got_x) if side < 2 else (face_y, got_y)
            code = nb_ref[0, 0, side, slot]
            near = local[side % 2, jnp.clip(code, 0, slots - 1)]
            far = got[turn][side % 2, jnp.clip(code - slots, 0, fcap - 1)]
            ghosts.append(jnp.where(code < 0, 0.0, jnp.where(code < slots, near, far)))
        west, east, south, north = ghosts
        has_above = here[2] + 1 < peers[2]
        fall = fall_ref[...].reshape(1, 1, bins)
        level = lax.broadcasted_iota(jnp.int32, (by, bz, bins), 1)
        rows = state[slot, pl.ds(0, by)]
        speed = speeds(wind, 0, 0)
        behind = west
        for x in range(bx):
            upward = jnp.maximum(speed, 0.0) * rows
            downward = jnp.minimum(speed, 0.0) * rows
            if x + 1 < bx:
                later = state[slot, pl.ds((x + 1) * by, by)]
                later_speed = speeds(wind, 0, x + 1)
                ahead = jnp.minimum(later_speed, 0.0) * later
            else:
                ahead = east
            total_x = (upward + ahead) - (behind + downward)
            speed_y = speeds(wind, 1, x)
            up_y = jnp.maximum(speed_y, 0.0) * rows
            down_y = jnp.minimum(speed_y, 0.0) * rows
            ahead_y = jnp.concatenate([down_y[1:], north[x][None]], axis=0)
            behind_y = jnp.concatenate([south[x][None], up_y[:-1]], axis=0)
            total_y = (up_y + ahead_y) - (behind_y + down_y)
            top = jnp.stack(
                [
                    jnp.broadcast_to(got_floor[turn][slot, x, pl.ds(y, 1), :], (bz, bins))
                    for y in range(by)
                ]
            )
            top = jnp.where(has_above, top, 0.0)
            upper = jnp.where(level == bz - 1, top, pltpu.roll(rows, bz - 1, 1))
            target[spot, pl.ds(x * by, by)] = rows - total_x - total_y - fall * (rows - upper)
            behind = upward
            if x + 1 < bx:
                rows, speed = later, later_speed
        turns = turns_ref[0, 0, 0, slot]
        size = step_time / jnp.maximum(jnp.full((1, bins), turns, jnp.int32), 1).astype(jnp.float32)

        half = cells // 2
        lead = [target[spot, pl.ds(i * half, half)].reshape(half * bz, bins) for i in (0, 1)]
        for index in range(most_turns):
            firsts = [product(mass, map_one) for mass in lead]
            lost, seconds = [], []
            for mass, first in zip(lead, firsts):
                parts = [first[:, i * bins : (i + 1) * bins] for i in range(6)]
                lost.append(mass * (parts[2] + parts[5]))
                paired = (parts[0] + parts[3]) * (parts[1] + parts[4])
                seconds.append(product(paired, map_two))
            lead = [
                jnp.where(
                    index < turns,
                    mass + size * (second[:, :bins] + second[:, bins:] - gone),
                    mass,
                )
                for mass, second, gone in zip(lead, seconds, lost)
            ]
        for i in (0, 1):
            target[spot, pl.ds(i * half, half)] = lead[i].reshape(half, bz, bins)

    def first_faces(slot, carry):
        fetch_mass(slot).wait()
        held = occupied_ref[0, 0, slot] > 0
        columns = wind_ref[0, 0, slot].reshape(2 * bx, by * bz).T
        for y in range(by):
            state[slot, cells, :, pl.ds(y * 2 * bx, 2 * bx)] = columns[y * bz : (y + 1) * bz]
        gather_faces(
            slot, lambda x: jnp.where(held, mass_ref[slot, pl.ds(x * by, by)], 0.0)
        )
        send_floor(0, slot)
        return carry

    lax.fori_loop(0, slots, first_faces, 0)
    copies = exchange(0, old_sends_ref)
    for fetch in fetches[1:6]:
        fetch.wait()
    for i, ref in enumerate((gain_a_ref, gain_b_ref, loss_k_ref)):
        for row in (0, bins):
            for part, values in enumerate(split(ref[...])):
                map_one[pl.ds(row, bins), pl.ds((part * 3 + i) * bins, bins)] = values
    for row in (0, bins):
        for part, values in enumerate(split(gain_c_ref[...])):
            map_two[pl.ds(row, bins), pl.ds(part * bins, bins)] = values
    await_faces(0)

    def move_copy(e):
        route = e // mcap
        west_leg = jnp.where(route == 1, 0, -1)
        north_leg = jnp.where(route == 0, 0, 1)
        there, inside = at((west_leg, north_leg, 0))
        _, incoming = at((-west_leg, -north_leg, 0))
        copy = pltpu.make_async_remote_copy(
            src_ref=parcel.at[e],
            dst_ref=arrived.at[e],
            send_sem=move_out.at[e],
            recv_sem=move_in.at[e],
            device_id=there,
            device_id_type=MESH,
        )
        return copy, inside, incoming

    def post(e, carry):
        copy, inside, _ = move_copy(e)
        parcel[e] = done[place[2, e]]
        pl.when(inside)(copy.start)
        return carry

    def first_step(spot, carry):
        slot = place[0, spot]
        step(0, slot, old_nb_ref, old_turns_ref, done, spot)
        done[spot, cells] = state[slot, cells]
        return carry

    def first_and_post(spot, carry):
        first_step(spot, carry)
        return post(spot, carry)

    shared = min(slots, entries)
    lax.fori_loop(0, shared, first_and_post, 0)
    if slots > shared:
        lax.fori_loop(shared, slots, first_step, 0)
    if entries > shared:
        lax.fori_loop(shared, entries, post, 0)
    await_sent(0, copies)

    def land(e, carry):
        copy, _, incoming = move_copy(e)
        pl.when(incoming)(copy.wait_recv)
        return carry

    lax.fori_loop(0, entries, land, 0)

    def second_faces(slot, carry):
        code = sources_ref[0, 0, slot]
        own = place[1, jnp.clip(code, 0, slots - 1)]
        came = jnp.clip(code - slots, 0, entries - 1)

        def choose(first, length):
            near = done[own, pl.ds(first, length)]
            far = arrived[came, pl.ds(first, length)]
            return jnp.where(code < 0, 0.0, jnp.where(code < slots, near, far))

        state[slot, cells] = choose(cells, 1)[0]
        gather_faces(slot, lambda x: choose(x * by, by))
        send_floor(1, slot)
        return carry

    lax.fori_loop(0, slots, second_faces, 0)
    copies = exchange(1, new_sends_ref)
    await_faces(1)

    def second_step(slot, carry):
        step(1, slot, new_nb_ref, new_turns_ref, out_ref, slot)
        return carry

    lax.fori_loop(0, slots, second_step, 0)
    await_sent(1, copies)

    def sent(e, carry):
        copy, inside, _ = move_copy(e)
        pl.when(inside)(copy.wait_send)
        return carry

    lax.fori_loop(0, entries, sent, 0)


def on_device(peers, bin_mass, wind_field, fall_speed, *rest):
    slots, bx, by, bz, bins = bin_mass.shape[2:]
    cells = bx * by
    old_sends, move_lists = rest[6], rest[8]
    fcap, mcap = old_sends.shape[-1], move_lists.shape[-1]
    entries = 3 * mcap
    small = [wind_field, fall_speed.reshape(1, bins), *rest]
    for i in (7, 12):
        small[i] = small[i].transpose(0, 1, 3, 2)
    for i in (8, 13):
        small[i] = small[i].transpose(0, 3, 1, 2)
    small[10] = small[10].transpose(0, 1, 3, 2)
    dims = (slots, bx, by, bz, bins, fcap, mcap, peers)
    vmem = pl.BlockSpec(memory_space=pltpu.VMEM)
    hbm = pl.BlockSpec(memory_space=pltpu.HBM)
    f32 = jnp.float32
    result = pl.pallas_call(
        functools.partial(kernel, dims),
        out_shape=jax.ShapeDtypeStruct((slots, cells, bz, bins), f32),
        in_specs=[hbm] * 16,
        out_specs=vmem,
        scratch_shapes=[
            pltpu.VMEM((slots, cells, bz, bins), f32),
            *[pltpu.VMEM(array.shape, f32) for array in small[:6]],
            *[pltpu.SMEM(array.shape, jnp.int32) for array in small[6:]],
            pltpu.SemaphoreType.DMA((slots,)),
            pltpu.SemaphoreType.DMA((len(small),)),
            pltpu.VMEM((slots, cells + 1, bz, bins), f32),
            pltpu.VMEM((slots, cells + 1, bz, bins), f32),
            pltpu.VMEM((entries, cells + 1, bz, bins), f32),
            pltpu.VMEM((entries, cells + 1, bz, bins), f32),
            pltpu.VMEM((2, slots, by, bz, bins), f32),
            pltpu.VMEM((2, slots, bx, bz, bins), f32),
            pltpu.VMEM((2, 2, fcap, by, bz, bins), f32),
            pltpu.VMEM((2, 2, fcap, bx, bz, bins), f32),
            pltpu.VMEM((2, fcap, by, bz, bins), f32),
            pltpu.VMEM((2, fcap, by, bz, bins), f32),
            pltpu.VMEM((2, fcap, bx, bz, bins), f32),
            pltpu.VMEM((2, fcap, bx, bz, bins), f32),
            pltpu.VMEM((slots, bx, by, bins), f32),
            pltpu.VMEM((slots, bx, by, bins), f32),
            pltpu.VMEM((slots, bx, by, bins), f32),
            pltpu.VMEM((2 * bins, 6 * bins), jnp.bfloat16),
            pltpu.VMEM((2 * bins, 2 * bins), jnp.bfloat16),
            pltpu.SMEM((3, max(slots, entries)), jnp.int32),
            pltpu.SemaphoreType.DMA((2, 4)),
            pltpu.SemaphoreType.DMA((2, 4)),
            pltpu.SemaphoreType.DMA((2, slots)),
            pltpu.SemaphoreType.DMA((2, slots)),
            pltpu.SemaphoreType.DMA((entries,)),
            pltpu.SemaphoreType.DMA((entries,)),
        ],
        compiler_params=pltpu.CompilerParams(
            collective_id=0, has_side_effects=True, vmem_limit_bytes=56 * 1024 * 1024
        ),
    )(
        bin_mass.reshape(slots, cells, bz, bins),
        *small,
    )
    return result.reshape(bin_mass.shape)


def solution(mesh):
    peers = tuple(mesh.shape[name] for name in ("gx", "gy", "gz"))
    placed = (
        P("gx", "gy", "gz", None, None, None, None),
        P("gx", "gy", "gz", None, None, None),
        P(),
        P(),
        P(),
        P(),
        P(),
        P("gx", "gy", None),
        P("gx", "gy", None, None),
        P("gx", "gy", None, None),
        P(None, "gx", "gy", "gz"),
        P("gx", "gy", None, None),
        P("gx", "gy", None),
        P("gx", "gy", None, None),
        P("gx", "gy", None, None),
        P(None, "gx", "gy", "gz"),
    )
    return jax.shard_map(
        functools.partial(on_device, peers),
        mesh=mesh,
        in_specs=placed,
        out_specs=P("gx", "gy", "gz", None, None, None, None),
        check_vma=False,
    )
```

```python
import functools

import jax
import jax.numpy as jnp
from jax import lax
from jax.experimental import pallas as pl
from jax.experimental.pallas import tpu as pltpu
from jax.sharding import PartitionSpec as P

step_time = 0.25
most_turns = 4
opposite = (1, 0, 3, 2)
MESH = pl.DeviceIdType.MESH


def split(values):
    high = values.astype(jnp.bfloat16)
    low = (values - high.astype(jnp.float32)).astype(jnp.bfloat16)
    return high, low


def product(rows, map_ref):
    return jnp.dot(
        jnp.concatenate(split(rows), axis=1), map_ref[...], preferred_element_type=jnp.float32
    )


def kernel(dims, *refs):
    far_mass, far_small, out_ref = refs[0], refs[1:16], refs[16]
    mass_ref, small_refs, (fetched_mass, fetched_small) = refs[17], refs[18:33], refs[33:35]
    wind_ref, fall_ref, gain_a_ref, gain_b_ref, gain_c_ref, loss_k_ref = small_refs[:6]
    occupied_ref, old_nb_ref, old_sends_ref, old_turns_ref, moves_ref = small_refs[6:11]
    sources_ref, new_nb_ref, new_sends_ref, new_turns_ref = small_refs[11:]
    state, done, parcel, arrived, face_x, face_y, send_x, send_y = refs[35:43]
    got_x_old, got_x_new, got_y_old, got_y_new, floor = refs[43:48]
    got_floor_old, got_floor_new, map_one, map_two, place = refs[48:53]
    face_out, face_in, floor_out, floor_in, move_out, move_in, final, delivered = refs[53:]
    slots, bx, by, bz, bins, fcap, mcap, peers = dims
    cells = bx * by
    entries = 3 * mcap
    got_x, got_y = (got_x_old, got_x_new), (got_y_old, got_y_new)
    got_floor = (got_floor_old, got_floor_new)
    here = tuple(lax.axis_index(name) for name in ("gx", "gy", "gz"))

    def at(shift):
        there = tuple(own + step for own, step in zip(here, shift))
        inside = True
        for spot, size in zip(there, peers):
            inside = inside & (spot >= 0) & (spot < size)
        return there, inside

    side_shift = ((-1, 0, 0), (1, 0, 0), (0, -1, 0), (0, 1, 0))
    route_shift = ((-1, 0, 0), (0, 1, 0), (-1, 1, 0))
    around = side_shift + ((0, 0, -1), (0, 0, 1), (-1, 1, 0), (1, -1, 0))

    def fetch_mass(slot):
        return pltpu.make_async_copy(
            far_mass.at[slot], mass_ref.at[slot], fetched_mass.at[slot]
        )

    fetches = [
        pltpu.make_async_copy(far, near, fetched_small.at[i])
        for i, (far, near) in enumerate(zip(far_small, small_refs))
    ]
    for fetch in fetches[6:] + fetches[:1]:
        fetch.start()
    for slot in range(slots):
        fetch_mass(slot).start()
    for fetch in fetches[1:6]:
        fetch.start()

    barrier = pltpu.get_barrier_semaphore()
    for shift in around:
        there, inside = at(shift)

        @pl.when(inside)
        def _():
            pl.semaphore_signal(barrier, inc=1, device_id=there, device_id_type=MESH)

    greeted = jnp.int32(0)
    for shift in around:
        greeted = greeted + at(shift)[1].astype(jnp.int32)
    pl.semaphore_wait(barrier, greeted)

    for fetch in fetches[6:] + fetches[:1]:
        fetch.wait()

    moved = [moves_ref[0, 0, e % mcap, e // mcap] for e in range(entries)]
    count = jnp.int32(0)
    rank = []
    for entry in moved:
        rank.append(count)
        count = count + (entry >= 0).astype(jnp.int32)
    where_to = []
    for slot in range(slots):
        spot = count
        goes = jnp.int32(0)
        for entry, spot_of in zip(moved, rank):
            spot = jnp.where(entry == slot, spot_of, spot)
            goes = jnp.where(entry == slot, 1, goes)
        count = count + (1 - goes)
        where_to.append(spot)
    for slot in range(slots):
        taken = jnp.int32(0)
        for other in range(slots):
            taken = jnp.where(where_to[other] == slot, other, taken)
        place[0, slot] = taken
        place[1, slot] = where_to[slot]
    for e in range(entries):
        place[2, e] = jnp.minimum(rank[e], slots - 1)

    def speeds(wind, component, x):
        return jnp.stack([speed_at(wind, component, x, y) for y in range(by)])

    def speed_at(wind, component, x, y):
        lane = (y * 2 + component) * bx + x
        return jnp.broadcast_to(wind[:, lane : lane + 1], (bz, bins))

    def gather_faces(slot, load_x):
        wind = state[slot, cells]
        for x in range(bx):
            rows = load_x(x)
            state[slot, pl.ds(x * by, by)] = rows
            for y in range(by):
                floor[slot, x, pl.ds(y, 1), :] = rows[y, 0:1, :]
            for y, side in ((by - 1, 0), (0, 1)):
                speed = speed_at(wind, 1, x, y)
                bounded = jnp.maximum(speed, 0.0) if side == 0 else jnp.minimum(speed, 0.0)
                face_y[side, slot, x] = bounded * rows[y]
            if x == bx - 1:
                face_x[0, slot] = jnp.maximum(speeds(wind, 0, x), 0.0) * rows
            if x == 0:
                face_x[1, slot] = jnp.minimum(speeds(wind, 0, x), 0.0) * rows

    def kept_at(turn, slot):
        held = jnp.clip(slot, 0, slots - 1)
        return place[1, held] if turn == 0 else held

    def exchange(turn, sends_ref):
        copies = []
        for side in range(4):
            local, out, got = (
                (face_x, send_x, got_x) if side < 2 else (face_y, send_y, got_y)
            )
            back = opposite[side]
            there, inside = at(side_shift[side])

            def pick(k, carry, side=side, local=local, out=out, back=back):
                entry = sends_ref[0, k, 0, side]
                rows = local[back % 2, kept_at(turn, entry)]
                out[turn, side % 2, k] = jnp.where(entry >= 0, rows, 0.0)
                return carry

            lax.fori_loop(0, fcap, pick, 0)
            copy = pltpu.make_async_remote_copy(
                src_ref=out.at[turn, side % 2],
                dst_ref=got[turn].at[back % 2],
                send_sem=face_out.at[turn, side],
                recv_sem=face_in.at[turn, back],
                device_id=there,
                device_id_type=MESH,
            )
            pl.when(inside)(copy.start)
            copies.append((copy, inside))
        return copies

    def floor_copy(turn, slot):
        return pltpu.make_async_remote_copy(
            src_ref=floor.at[slot],
            dst_ref=got_floor[turn].at[slot],
            send_sem=floor_out.at[turn, slot],
            recv_sem=floor_in.at[turn, slot],
            device_id=at((0, 0, -1))[0],
            device_id_type=MESH,
        )

    def send_floor(turn, slot):
        pl.when(at((0, 0, -1))[1])(floor_copy(turn, slot).start)

    def await_faces(turn):
        for side in range(4):
            _, inside = at(side_shift[side])
            got = got_x if side < 2 else got_y
            landing = pltpu.make_async_remote_copy(
                src_ref=got[turn].at[side % 2],
                dst_ref=got[turn].at[side % 2],
                send_sem=face_out.at[turn, side],
                recv_sem=face_in.at[turn, side],
                device_id=at(side_shift[side])[0],
                device_id_type=MESH,
            )
            pl.when(inside)(landing.wait_recv)

    def await_sent(turn, copies):
        for copy, inside in copies:
            pl.when(inside)(copy.wait_send)

        @pl.when(at((0, 0, -1))[1])
        def _():
            for slot in range(slots):
                floor_copy(turn, slot).wait_send()

    def step(turn, slot, nb_ref, turns_ref, target, spot):
        wind = state[spot, cells]
        has_above = here[2] + 1 < peers[2]
        pl.when(has_above)(floor_copy(turn, spot).wait_recv)
        ghosts = []
        for side in range(4):
            local, got = (face_x, got_x) if side < 2 else (face_y, got_y)
            code = nb_ref[0, 0, side, slot]
            near = local[side % 2, kept_at(turn, code)]
            far = got[turn][side % 2, jnp.clip(code - slots, 0, fcap - 1)]
            ghosts.append(jnp.where(code < 0, 0.0, jnp.where(code < slots, near, far)))
        west, east, south, north = ghosts
        fall = fall_ref[...].reshape(1, 1, bins)
        level = lax.broadcasted_iota(jnp.int32, (by, bz, bins), 1)
        rows = state[spot, pl.ds(0, by)]
        speed = speeds(wind, 0, 0)
        behind = west
        for x in range(bx):
            upward = jnp.maximum(speed, 0.0) * rows
            downward = jnp.minimum(speed, 0.0) * rows
            if x + 1 < bx:
                later = state[spot, pl.ds((x + 1) * by, by)]
                later_speed = speeds(wind, 0, x + 1)
                ahead = jnp.minimum(later_speed, 0.0) * later
            else:
                ahead = east
            total_x = (upward + ahead) - (behind + downward)
            speed_y = speeds(wind, 1, x)
            up_y = jnp.maximum(speed_y, 0.0) * rows
            down_y = jnp.minimum(speed_y, 0.0) * rows
            ahead_y = jnp.concatenate([down_y[1:], north[x][None]], axis=0)
            behind_y = jnp.concatenate([south[x][None], up_y[:-1]], axis=0)
            total_y = (up_y + ahead_y) - (behind_y + down_y)
            top = jnp.stack(
                [
                    jnp.broadcast_to(got_floor[turn][spot, x, pl.ds(y, 1), :], (bz, bins))
                    for y in range(by)
                ]
            )
            top = jnp.where(has_above, top, 0.0)
            upper = jnp.where(level == bz - 1, top, pltpu.roll(rows, bz - 1, 1))
            target[spot, pl.ds(x * by, by)] = rows - total_x - total_y - fall * (rows - upper)
            behind = upward
            if x + 1 < bx:
                rows, speed = later, later_speed
        turns = turns_ref[0, 0, 0, slot]
        size = step_time / jnp.maximum(jnp.full((1, bins), turns, jnp.int32), 1).astype(jnp.float32)

        half = cells // 2
        lead = [target[spot, pl.ds(i * half, half)].reshape(half * bz, bins) for i in (0, 1)]
        for index in range(most_turns):
            firsts = [product(mass, map_one) for mass in lead]
            lost, seconds = [], []
            for mass, first in zip(lead, firsts):
                parts = [first[:, i * bins : (i + 1) * bins] for i in range(6)]
                lost.append(mass * (parts[2] + parts[5]))
                paired = (parts[0] + parts[3]) * (parts[1] + parts[4])
                seconds.append(product(paired, map_two))
            lead = [
                jnp.where(
                    index < turns,
                    mass + size * (second[:, :bins] + second[:, bins:] - gone),
                    mass,
                )
                for mass, second, gone in zip(lead, seconds, lost)
            ]
        for i in (0, 1):
            target[spot, pl.ds(i * half, half)] = lead[i].reshape(half, bz, bins)

    def first_faces(spot, carry):
        slot = place[0, spot]
        held = occupied_ref[0, 0, slot] > 0
        columns = wind_ref[0, 0, slot].reshape(2 * bx, by * bz).T
        for y in range(by):
            state[spot, cells, :, pl.ds(y * 2 * bx, 2 * bx)] = columns[y * bz : (y + 1) * bz]
        gather_faces(
            spot, lambda x: jnp.where(held, mass_ref[slot, pl.ds(x * by, by)], 0.0)
        )
        send_floor(0, spot)
        return carry

    for slot in range(slots):
        fetch_mass(slot).wait()
    lax.fori_loop(0, slots, first_faces, 0)
    copies = exchange(0, old_sends_ref)
    for fetch in fetches[1:6]:
        fetch.wait()
    for i, ref in enumerate((gain_a_ref, gain_b_ref, loss_k_ref)):
        for row in (0, bins):
            for part, values in enumerate(split(ref[...])):
                map_one[pl.ds(row, bins), pl.ds((part * 3 + i) * bins, bins)] = values
    for row in (0, bins):
        for part, values in enumerate(split(gain_c_ref[...])):
            map_two[pl.ds(row, bins), pl.ds(part * bins, bins)] = values
    await_faces(0)

    def move_copy(e):
        route = e // mcap
        west_leg = jnp.where(route == 1, 0, -1)
        north_leg = jnp.where(route == 0, 0, 1)
        there, inside = at((west_leg, north_leg, 0))
        _, incoming = at((-west_leg, -north_leg, 0))
        copy = pltpu.make_async_remote_copy(
            src_ref=parcel.at[e],
            dst_ref=arrived.at[e],
            send_sem=move_out.at[e],
            recv_sem=move_in.at[e],
            device_id=there,
            device_id_type=MESH,
        )
        return copy, inside, incoming

    def post(e, carry):
        copy, inside, _ = move_copy(e)
        parcel[e] = done[place[2, e]]
        pl.when(inside)(copy.start)
        return carry

    def first_step(spot, carry):
        slot = place[0, spot]
        step(0, slot, old_nb_ref, old_turns_ref, done, spot)
        done[spot, cells] = state[spot, cells]
        return carry

    def first_and_post(spot, carry):
        first_step(spot, carry)
        return post(spot, carry)

    shared = min(slots, entries)
    lax.fori_loop(0, shared, first_and_post, 0)
    if slots > shared:
        lax.fori_loop(shared, slots, first_step, 0)
    if entries > shared:
        lax.fori_loop(shared, entries, post, 0)
    await_sent(0, copies)

    def land(e, carry):
        copy, _, incoming = move_copy(e)
        pl.when(incoming)(copy.wait_recv)
        return carry

    lax.fori_loop(0, entries, land, 0)

    def second_faces(slot, carry):
        code = sources_ref[0, 0, slot]
        own = place[1, jnp.clip(code, 0, slots - 1)]
        came = jnp.clip(code - slots, 0, entries - 1)

        def choose(first, length):
            near = done[own, pl.ds(first, length)]
            far = arrived[came, pl.ds(first, length)]
            return jnp.where(code < 0, 0.0, jnp.where(code < slots, near, far))

        state[slot, cells] = choose(cells, 1)[0]
        gather_faces(slot, lambda x: choose(x * by, by))
        send_floor(1, slot)
        return carry

    lax.fori_loop(0, slots, second_faces, 0)
    copies = exchange(1, new_sends_ref)
    await_faces(1)

    def second_step(slot, carry):
        step(1, slot, new_nb_ref, new_turns_ref, final, slot)
        deliver(slot).start()
        return carry

    def deliver(slot):
        return pltpu.make_async_copy(final.at[slot], out_ref.at[slot], delivered.at[slot])

    lax.fori_loop(0, slots, second_step, 0)
    for slot in range(slots):
        deliver(slot).wait()
    await_sent(1, copies)

    def sent(e, carry):
        copy, inside, _ = move_copy(e)
        pl.when(inside)(copy.wait_send)
        return carry

    lax.fori_loop(0, entries, sent, 0)


def on_device(peers, bin_mass, wind_field, fall_speed, *rest):
    slots, bx, by, bz, bins = bin_mass.shape[2:]
    cells = bx * by
    old_sends, move_lists = rest[6], rest[8]
    fcap, mcap = old_sends.shape[-1], move_lists.shape[-1]
    entries = 3 * mcap
    small = [wind_field, fall_speed.reshape(1, bins), *rest]
    for i in (7, 12):
        small[i] = small[i].transpose(0, 1, 3, 2)
    for i in (8, 13):
        small[i] = small[i].transpose(0, 3, 1, 2)
    small[10] = small[10].transpose(0, 1, 3, 2)
    dims = (slots, bx, by, bz, bins, fcap, mcap, peers)
    hbm = pl.BlockSpec(memory_space=pltpu.HBM)
    f32 = jnp.float32
    result = pl.pallas_call(
        functools.partial(kernel, dims),
        out_shape=jax.ShapeDtypeStruct((slots, cells, bz, bins), f32),
        in_specs=[hbm] * 16,
        out_specs=hbm,
        scratch_shapes=[
            pltpu.VMEM((slots, cells, bz, bins), f32),
            *[pltpu.VMEM(array.shape, f32) for array in small[:6]],
            *[pltpu.SMEM(array.shape, jnp.int32) for array in small[6:]],
            pltpu.SemaphoreType.DMA((slots,)),
            pltpu.SemaphoreType.DMA((len(small),)),
            pltpu.VMEM((slots, cells + 1, bz, bins), f32),
            pltpu.VMEM((slots, cells + 1, bz, bins), f32),
            pltpu.VMEM((entries, cells + 1, bz, bins), f32),
            pltpu.VMEM((entries, cells + 1, bz, bins), f32),
            pltpu.VMEM((2, slots, by, bz, bins), f32),
            pltpu.VMEM((2, slots, bx, bz, bins), f32),
            pltpu.VMEM((2, 2, fcap, by, bz, bins), f32),
            pltpu.VMEM((2, 2, fcap, bx, bz, bins), f32),
            pltpu.VMEM((2, fcap, by, bz, bins), f32),
            pltpu.VMEM((2, fcap, by, bz, bins), f32),
            pltpu.VMEM((2, fcap, bx, bz, bins), f32),
            pltpu.VMEM((2, fcap, bx, bz, bins), f32),
            pltpu.VMEM((slots, bx, by, bins), f32),
            pltpu.VMEM((slots, bx, by, bins), f32),
            pltpu.VMEM((slots, bx, by, bins), f32),
            pltpu.VMEM((2 * bins, 6 * bins), jnp.bfloat16),
            pltpu.VMEM((2 * bins, 2 * bins), jnp.bfloat16),
            pltpu.SMEM((3, max(slots, entries)), jnp.int32),
            pltpu.SemaphoreType.DMA((2, 4)),
            pltpu.SemaphoreType.DMA((2, 4)),
            pltpu.SemaphoreType.DMA((2, slots)),
            pltpu.SemaphoreType.DMA((2, slots)),
            pltpu.SemaphoreType.DMA((entries,)),
            pltpu.SemaphoreType.DMA((entries,)),
            pltpu.VMEM((slots, cells, bz, bins), f32),
            pltpu.SemaphoreType.DMA((slots,)),
        ],
        compiler_params=pltpu.CompilerParams(
            collective_id=0, has_side_effects=True, vmem_limit_bytes=56 * 1024 * 1024
        ),
    )(
        bin_mass.reshape(slots, cells, bz, bins),
        *small,
    )
    return result.reshape(bin_mass.shape)


def solution(mesh):
    peers = tuple(mesh.shape[name] for name in ("gx", "gy", "gz"))
    placed = (
        P("gx", "gy", "gz", None, None, None, None),
        P("gx", "gy", "gz", None, None, None),
        P(),
        P(),
        P(),
        P(),
        P(),
        P("gx", "gy", None),
        P("gx", "gy", None, None),
        P("gx", "gy", None, None),
        P(None, "gx", "gy", "gz"),
        P("gx", "gy", None, None),
        P("gx", "gy", None),
        P("gx", "gy", None, None),
        P("gx", "gy", None, None),
        P(None, "gx", "gy", "gz"),
    )
    return jax.shard_map(
        functools.partial(on_device, peers),
        mesh=mesh,
        in_specs=placed,
        out_specs=P("gx", "gy", "gz", None, None, None, None),
        check_vma=False,
    )
```

```python
import functools

import jax
import jax.numpy as jnp
from jax import lax
from jax.experimental import pallas as pl
from jax.experimental.pallas import tpu as pltpu
from jax.sharding import PartitionSpec as P

step_time = 0.25
most_turns = 4
opposite = (1, 0, 3, 2)
MESH = pl.DeviceIdType.MESH


def split(values):
    high = values.astype(jnp.bfloat16)
    low = (values - high.astype(jnp.float32)).astype(jnp.bfloat16)
    return high, low


def product(rows, map_ref):
    return jnp.dot(
        jnp.concatenate(split(rows), axis=1), map_ref[...], preferred_element_type=jnp.float32
    )


def kernel(dims, *refs):
    far_mass, far_small, out_ref = refs[0], refs[1:16], refs[16]
    mass_ref, small_refs, (fetched_mass, fetched_small) = refs[17], refs[18:33], refs[33:35]
    wind_ref, fall_ref, gain_a_ref, gain_b_ref, gain_c_ref, loss_k_ref = small_refs[:6]
    occupied_ref, old_nb_ref, old_sends_ref, old_turns_ref, moves_ref = small_refs[6:11]
    sources_ref, new_nb_ref, new_sends_ref, new_turns_ref = small_refs[11:]
    state, done, parcel, arrived, face_x, face_y, send_x, send_y = refs[35:43]
    got_x_old, got_x_new, got_y_old, got_y_new, floor = refs[43:48]
    got_floor_old, got_floor_new, map_one, map_two, place = refs[48:53]
    face_out, face_in, floor_out, floor_in, move_out, move_in, final, delivered = refs[53:]
    slots, bx, by, bz, bins, fcap, mcap, peers = dims
    cells = bx * by
    entries = 3 * mcap
    got_x, got_y = (got_x_old, got_x_new), (got_y_old, got_y_new)
    got_floor = (got_floor_old, got_floor_new)
    here = tuple(lax.axis_index(name) for name in ("gx", "gy", "gz"))

    def at(shift):
        there = tuple(own + step for own, step in zip(here, shift))
        inside = True
        for spot, size in zip(there, peers):
            inside = inside & (spot >= 0) & (spot < size)
        return there, inside

    side_shift = ((-1, 0, 0), (1, 0, 0), (0, -1, 0), (0, 1, 0))
    route_shift = ((-1, 0, 0), (0, 1, 0), (-1, 1, 0))
    around = side_shift + ((0, 0, -1), (0, 0, 1), (-1, 1, 0), (1, -1, 0))

    def fetch_mass(slot):
        return pltpu.make_async_copy(
            far_mass.at[slot], mass_ref.at[slot], fetched_mass.at[slot]
        )

    fetches = [
        pltpu.make_async_copy(far, near, fetched_small.at[i])
        for i, (far, near) in enumerate(zip(far_small, small_refs))
    ]
    for fetch in fetches[6:] + fetches[:1]:
        fetch.start()
    for slot in range(slots):
        fetch_mass(slot).start()
    for fetch in fetches[1:6]:
        fetch.start()

    barrier = pltpu.get_barrier_semaphore()
    for shift in around:
        there, inside = at(shift)

        @pl.when(inside)
        def _():
            pl.semaphore_signal(barrier, inc=1, device_id=there, device_id_type=MESH)

    greeted = jnp.int32(0)
    for shift in around:
        greeted = greeted + at(shift)[1].astype(jnp.int32)
    pl.semaphore_wait(barrier, greeted)

    for fetch in fetches[6:] + fetches[:1]:
        fetch.wait()

    def entry_at(turn):
        route = turn // mcap
        turned = jnp.where(route < 2, 1 - route, route)
        return jnp.where(here[2] % 2 == 0, route, turned), turn % mcap

    moved = []
    for turn in range(entries):
        route, k = entry_at(turn)
        moved.append(moves_ref[0, 0, k, route])
    count = jnp.int32(0)
    rank = []
    for entry in moved:
        rank.append(count)
        count = count + (entry >= 0).astype(jnp.int32)
    where_to = []
    for slot in range(slots):
        spot = count
        goes = jnp.int32(0)
        for entry, spot_of in zip(moved, rank):
            spot = jnp.where(entry == slot, spot_of, spot)
            goes = jnp.where(entry == slot, 1, goes)
        count = count + (1 - goes)
        where_to.append(spot)
    for slot in range(slots):
        taken = jnp.int32(0)
        for other in range(slots):
            taken = jnp.where(where_to[other] == slot, other, taken)
        place[0, slot] = taken
        place[1, slot] = where_to[slot]
    for e in range(entries):
        place[2, e] = jnp.minimum(rank[e], slots - 1)

    def speeds(wind, component, x):
        return jnp.stack([speed_at(wind, component, x, y) for y in range(by)])

    def speed_at(wind, component, x, y):
        lane = (y * 2 + component) * bx + x
        return jnp.broadcast_to(wind[:, lane : lane + 1], (bz, bins))

    def gather_faces(slot, load_x):
        wind = state[slot, cells]
        for x in range(bx):
            rows = load_x(x)
            state[slot, pl.ds(x * by, by)] = rows
            for y in range(by):
                floor[slot, x, pl.ds(y, 1), :] = rows[y, 0:1, :]
            for y, side in ((by - 1, 0), (0, 1)):
                speed = speed_at(wind, 1, x, y)
                bounded = jnp.maximum(speed, 0.0) if side == 0 else jnp.minimum(speed, 0.0)
                face_y[side, slot, x] = bounded * rows[y]
            if x == bx - 1:
                face_x[0, slot] = jnp.maximum(speeds(wind, 0, x), 0.0) * rows
            if x == 0:
                face_x[1, slot] = jnp.minimum(speeds(wind, 0, x), 0.0) * rows

    def exchange(turn, sends_ref):
        copies = []
        for side in range(4):
            local, out, got = (
                (face_x, send_x, got_x) if side < 2 else (face_y, send_y, got_y)
            )
            back = opposite[side]
            there, inside = at(side_shift[side])

            def pick(k, carry, side=side, local=local, out=out, back=back):
                entry = sends_ref[0, k, 0, side]
                rows = local[back % 2, jnp.clip(entry, 0, slots - 1)]
                out[turn, side % 2, k] = jnp.where(entry >= 0, rows, 0.0)
                return carry

            lax.fori_loop(0, fcap, pick, 0)
            copy = pltpu.make_async_remote_copy(
                src_ref=out.at[turn, side % 2],
                dst_ref=got[turn].at[back % 2],
                send_sem=face_out.at[turn, side],
                recv_sem=face_in.at[turn, back],
                device_id=there,
                device_id_type=MESH,
            )
            pl.when(inside)(copy.start)
            copies.append((copy, inside))
        return copies

    def floor_copy(turn, slot):
        return pltpu.make_async_remote_copy(
            src_ref=floor.at[slot],
            dst_ref=got_floor[turn].at[slot],
            send_sem=floor_out.at[turn, slot],
            recv_sem=floor_in.at[turn, slot],
            device_id=at((0, 0, -1))[0],
            device_id_type=MESH,
        )

    def send_floor(turn, slot):
        pl.when(at((0, 0, -1))[1])(floor_copy(turn, slot).start)

    def await_faces(turn):
        _, above_inside = at((0, 0, 1))
        for side in range(4):
            _, inside = at(side_shift[side])
            got = got_x if side < 2 else got_y
            landing = pltpu.make_async_remote_copy(
                src_ref=got[turn].at[side % 2],
                dst_ref=got[turn].at[side % 2],
                send_sem=face_out.at[turn, side],
                recv_sem=face_in.at[turn, side],
                device_id=at(side_shift[side])[0],
                device_id_type=MESH,
            )
            pl.when(inside)(landing.wait_recv)

        @pl.when(above_inside)
        def _():
            for slot in range(slots):
                floor_copy(turn, slot).wait_recv()

    def await_sent(turn, copies):
        for copy, inside in copies:
            pl.when(inside)(copy.wait_send)

        @pl.when(at((0, 0, -1))[1])
        def _():
            for slot in range(slots):
                floor_copy(turn, slot).wait_send()

    def step(turn, slot, nb_ref, turns_ref, target, spot):
        wind = state[slot, cells]
        ghosts = []
        for side in range(4):
            local, got = (face_x, got_x) if side < 2 else (face_y, got_y)
            code = nb_ref[0, 0, side, slot]
            near = local[side % 2, jnp.clip(code, 0, slots - 1)]
            far = got[turn][side % 2, jnp.clip(code - slots, 0, fcap - 1)]
            ghosts.append(jnp.where(code < 0, 0.0, jnp.where(code < slots, near, far)))
        west, east, south, north = ghosts
        has_above = here[2] + 1 < peers[2]
        fall = fall_ref[...].reshape(1, 1, bins)
        level = lax.broadcasted_iota(jnp.int32, (by, bz, bins), 1)
        rows = state[slot, pl.ds(0, by)]
        speed = speeds(wind, 0, 0)
        behind = west
        for x in range(bx):
            upward = jnp.maximum(speed, 0.0) * rows
            downward = jnp.minimum(speed, 0.0) * rows
            if x + 1 < bx:
                later = state[slot, pl.ds((x + 1) * by, by)]
                later_speed = speeds(wind, 0, x + 1)
                ahead = jnp.minimum(later_speed, 0.0) * later
            else:
                ahead = east
            total_x = (upward + ahead) - (behind + downward)
            speed_y = speeds(wind, 1, x)
            up_y = jnp.maximum(speed_y, 0.0) * rows
            down_y = jnp.minimum(speed_y, 0.0) * rows
            ahead_y = jnp.concatenate([down_y[1:], north[x][None]], axis=0)
            behind_y = jnp.concatenate([south[x][None], up_y[:-1]], axis=0)
            total_y = (up_y + ahead_y) - (behind_y + down_y)
            top = jnp.stack(
                [
                    jnp.broadcast_to(got_floor[turn][slot, x, pl.ds(y, 1), :], (bz, bins))
                    for y in range(by)
                ]
            )
            top = jnp.where(has_above, top, 0.0)
            upper = jnp.where(level == bz - 1, top, pltpu.roll(rows, bz - 1, 1))
            target[spot, pl.ds(x * by, by)] = rows - total_x - total_y - fall * (rows - upper)
            behind = upward
            if x + 1 < bx:
                rows, speed = later, later_speed
        turns = turns_ref[0, 0, 0, slot]
        size = step_time / jnp.maximum(jnp.full((1, bins), turns, jnp.int32), 1).astype(jnp.float32)

        half = cells // 2
        lead = [target[spot, pl.ds(i * half, half)].reshape(half * bz, bins) for i in (0, 1)]
        for index in range(most_turns):
            firsts = [product(mass, map_one) for mass in lead]
            lost, seconds = [], []
            for mass, first in zip(lead, firsts):
                parts = [first[:, i * bins : (i + 1) * bins] for i in range(6)]
                lost.append(mass * (parts[2] + parts[5]))
                paired = (parts[0] + parts[3]) * (parts[1] + parts[4])
                seconds.append(product(paired, map_two))
            lead = [
                jnp.where(
                    index < turns,
                    mass + size * (second[:, :bins] + second[:, bins:] - gone),
                    mass,
                )
                for mass, second, gone in zip(lead, seconds, lost)
            ]
        for i in (0, 1):
            target[spot, pl.ds(i * half, half)] = lead[i].reshape(half, bz, bins)

    def first_faces(slot, carry):
        fetch_mass(slot).wait()
        held = occupied_ref[0, 0, slot] > 0
        columns = wind_ref[0, 0, slot].reshape(2 * bx, by * bz).T
        for y in range(by):
            state[slot, cells, :, pl.ds(y * 2 * bx, 2 * bx)] = columns[y * bz : (y + 1) * bz]
        gather_faces(
            slot, lambda x: jnp.where(held, mass_ref[slot, pl.ds(x * by, by)], 0.0)
        )
        send_floor(0, slot)
        return carry

    lax.fori_loop(0, slots, first_faces, 0)
    copies = exchange(0, old_sends_ref)
    for fetch in fetches[1:6]:
        fetch.wait()
    for i, ref in enumerate((gain_a_ref, gain_b_ref, loss_k_ref)):
        for row in (0, bins):
            for part, values in enumerate(split(ref[...])):
                map_one[pl.ds(row, bins), pl.ds((part * 3 + i) * bins, bins)] = values
    for row in (0, bins):
        for part, values in enumerate(split(gain_c_ref[...])):
            map_two[pl.ds(row, bins), pl.ds(part * bins, bins)] = values
    await_faces(0)

    def move_copy(e):
        route = e // mcap
        west_leg = jnp.where(route == 1, 0, -1)
        north_leg = jnp.where(route == 0, 0, 1)
        there, inside = at((west_leg, north_leg, 0))
        _, incoming = at((-west_leg, -north_leg, 0))
        copy = pltpu.make_async_remote_copy(
            src_ref=parcel.at[e],
            dst_ref=arrived.at[e],
            send_sem=move_out.at[e],
            recv_sem=move_in.at[e],
            device_id=there,
            device_id_type=MESH,
        )
        return copy, inside, incoming

    def post(turn, carry):
        route, k = entry_at(turn)
        e = route * mcap + k
        copy, inside, _ = move_copy(e)
        parcel[e] = done[place[2, turn]]
        pl.when(inside)(copy.start)
        return carry

    def first_step(spot, carry):
        slot = place[0, spot]
        step(0, slot, old_nb_ref, old_turns_ref, done, spot)
        done[spot, cells] = state[slot, cells]
        return carry

    def first_and_post(spot, carry):
        first_step(spot, carry)
        return post(spot, carry)

    shared = min(slots, entries)
    lax.fori_loop(0, shared, first_and_post, 0)
    if slots > shared:
        lax.fori_loop(shared, slots, first_step, 0)
    if entries > shared:
        lax.fori_loop(shared, entries, post, 0)
    await_sent(0, copies)

    def land(e, carry):
        copy, _, incoming = move_copy(e)
        pl.when(incoming)(copy.wait_recv)
        return carry

    lax.fori_loop(0, entries, land, 0)

    def second_faces(slot, carry):
        code = sources_ref[0, 0, slot]
        own = place[1, jnp.clip(code, 0, slots - 1)]
        came = jnp.clip(code - slots, 0, entries - 1)

        def choose(first, length):
            near = done[own, pl.ds(first, length)]
            far = arrived[came, pl.ds(first, length)]
            return jnp.where(code < 0, 0.0, jnp.where(code < slots, near, far))

        state[slot, cells] = choose(cells, 1)[0]
        gather_faces(slot, lambda x: choose(x * by, by))
        send_floor(1, slot)
        return carry

    lax.fori_loop(0, slots, second_faces, 0)
    copies = exchange(1, new_sends_ref)
    await_faces(1)

    def second_step(slot, carry):
        step(1, slot, new_nb_ref, new_turns_ref, final, slot)
        deliver(slot).start()
        return carry

    def deliver(slot):
        return pltpu.make_async_copy(final.at[slot], out_ref.at[slot], delivered.at[slot])

    lax.fori_loop(0, slots, second_step, 0)
    for slot in range(slots):
        deliver(slot).wait()
    await_sent(1, copies)

    def sent(e, carry):
        copy, inside, _ = move_copy(e)
        pl.when(inside)(copy.wait_send)
        return carry

    lax.fori_loop(0, entries, sent, 0)


def on_device(peers, bin_mass, wind_field, fall_speed, *rest):
    slots, bx, by, bz, bins = bin_mass.shape[2:]
    cells = bx * by
    old_sends, move_lists = rest[6], rest[8]
    fcap, mcap = old_sends.shape[-1], move_lists.shape[-1]
    entries = 3 * mcap
    small = [wind_field, fall_speed.reshape(1, bins), *rest]
    for i in (7, 12):
        small[i] = small[i].transpose(0, 1, 3, 2)
    for i in (8, 13):
        small[i] = small[i].transpose(0, 3, 1, 2)
    small[10] = small[10].transpose(0, 1, 3, 2)
    dims = (slots, bx, by, bz, bins, fcap, mcap, peers)
    hbm = pl.BlockSpec(memory_space=pltpu.HBM)
    f32 = jnp.float32
    result = pl.pallas_call(
        functools.partial(kernel, dims),
        out_shape=jax.ShapeDtypeStruct((slots, cells, bz, bins), f32),
        in_specs=[hbm] * 16,
        out_specs=hbm,
        scratch_shapes=[
            pltpu.VMEM((slots, cells, bz, bins), f32),
            *[pltpu.VMEM(array.shape, f32) for array in small[:6]],
            *[pltpu.SMEM(array.shape, jnp.int32) for array in small[6:]],
            pltpu.SemaphoreType.DMA((slots,)),
            pltpu.SemaphoreType.DMA((len(small),)),
            pltpu.VMEM((slots, cells + 1, bz, bins), f32),
            pltpu.VMEM((slots, cells + 1, bz, bins), f32),
            pltpu.VMEM((entries, cells + 1, bz, bins), f32),
            pltpu.VMEM((entries, cells + 1, bz, bins), f32),
            pltpu.VMEM((2, slots, by, bz, bins), f32),
            pltpu.VMEM((2, slots, bx, bz, bins), f32),
            pltpu.VMEM((2, 2, fcap, by, bz, bins), f32),
            pltpu.VMEM((2, 2, fcap, bx, bz, bins), f32),
            pltpu.VMEM((2, fcap, by, bz, bins), f32),
            pltpu.VMEM((2, fcap, by, bz, bins), f32),
            pltpu.VMEM((2, fcap, bx, bz, bins), f32),
            pltpu.VMEM((2, fcap, bx, bz, bins), f32),
            pltpu.VMEM((slots, bx, by, bins), f32),
            pltpu.VMEM((slots, bx, by, bins), f32),
            pltpu.VMEM((slots, bx, by, bins), f32),
            pltpu.VMEM((2 * bins, 6 * bins), jnp.bfloat16),
            pltpu.VMEM((2 * bins, 2 * bins), jnp.bfloat16),
            pltpu.SMEM((3, max(slots, entries)), jnp.int32),
            pltpu.SemaphoreType.DMA((2, 4)),
            pltpu.SemaphoreType.DMA((2, 4)),
            pltpu.SemaphoreType.DMA((2, slots)),
            pltpu.SemaphoreType.DMA((2, slots)),
            pltpu.SemaphoreType.DMA((entries,)),
            pltpu.SemaphoreType.DMA((entries,)),
            pltpu.VMEM((slots, cells, bz, bins), f32),
            pltpu.SemaphoreType.DMA((slots,)),
        ],
        compiler_params=pltpu.CompilerParams(
            collective_id=0, has_side_effects=True, vmem_limit_bytes=56 * 1024 * 1024
        ),
    )(
        bin_mass.reshape(slots, cells, bz, bins),
        *small,
    )
    return result.reshape(bin_mass.shape)


def solution(mesh):
    peers = tuple(mesh.shape[name] for name in ("gx", "gy", "gz"))
    placed = (
        P("gx", "gy", "gz", None, None, None, None),
        P("gx", "gy", "gz", None, None, None),
        P(),
        P(),
        P(),
        P(),
        P(),
        P("gx", "gy", None),
        P("gx", "gy", None, None),
        P("gx", "gy", None, None),
        P(None, "gx", "gy", "gz"),
        P("gx", "gy", None, None),
        P("gx", "gy", None),
        P("gx", "gy", None, None),
        P("gx", "gy", None, None),
        P(None, "gx", "gy", "gz"),
    )
    return jax.shard_map(
        functools.partial(on_device, peers),
        mesh=mesh,
        in_specs=placed,
        out_specs=P("gx", "gy", "gz", None, None, None, None),
        check_vma=False,
    )
```

```python
import functools

import jax
import jax.numpy as jnp
from jax import lax
from jax.experimental import pallas as pl
from jax.experimental.pallas import tpu as pltpu
from jax.sharding import PartitionSpec as P

step_time = 0.25
most_turns = 4
opposite = (1, 0, 3, 2)
MESH = pl.DeviceIdType.MESH


def split(values):
    high = values.astype(jnp.bfloat16)
    low = (values - high.astype(jnp.float32)).astype(jnp.bfloat16)
    return high, low


def product(rows, map_ref):
    return jnp.dot(
        jnp.concatenate(split(rows), axis=1), map_ref[...], preferred_element_type=jnp.float32
    )


def kernel(dims, *refs):
    far_mass, far_small, out_ref = refs[0], refs[1:16], refs[16]
    mass_ref, small_refs, (fetched_mass, fetched_small) = refs[17], refs[18:33], refs[33:35]
    wind_ref, fall_ref, gain_a_ref, gain_b_ref, gain_c_ref, loss_k_ref = small_refs[:6]
    occupied_ref, old_nb_ref, old_sends_ref, old_turns_ref, moves_ref = small_refs[6:11]
    sources_ref, new_nb_ref, new_sends_ref, new_turns_ref = small_refs[11:]
    state, done, parcel, arrived, face_x, face_y, send_x, send_y = refs[35:43]
    got_x_old, got_x_new, got_y_old, got_y_new, floor = refs[43:48]
    got_floor_old, got_floor_new, map_one, map_two, place = refs[48:53]
    face_out, face_in, floor_out, floor_in, move_out, move_in, final, delivered = refs[53:]
    slots, bx, by, bz, bins, fcap, mcap, peers = dims
    cells = bx * by
    entries = 3 * mcap
    got_x, got_y = (got_x_old, got_x_new), (got_y_old, got_y_new)
    got_floor = (got_floor_old, got_floor_new)
    here = tuple(lax.axis_index(name) for name in ("gx", "gy", "gz"))

    def at(shift):
        there = tuple(own + step for own, step in zip(here, shift))
        inside = True
        for spot, size in zip(there, peers):
            inside = inside & (spot >= 0) & (spot < size)
        return there, inside

    side_shift = ((-1, 0, 0), (1, 0, 0), (0, -1, 0), (0, 1, 0))
    route_shift = ((-1, 0, 0), (0, 1, 0), (-1, 1, 0))
    around = side_shift + ((0, 0, -1), (0, 0, 1), (-1, 1, 0), (1, -1, 0))

    def fetch_mass(slot):
        return pltpu.make_async_copy(
            far_mass.at[slot], mass_ref.at[slot], fetched_mass.at[slot]
        )

    fetches = [
        pltpu.make_async_copy(far, near, fetched_small.at[i])
        for i, (far, near) in enumerate(zip(far_small, small_refs))
    ]
    for fetch in fetches[6:] + fetches[:1]:
        fetch.start()
    for slot in range(slots):
        fetch_mass(slot).start()
    for fetch in fetches[1:6]:
        fetch.start()

    barrier = pltpu.get_barrier_semaphore()
    for shift in around:
        there, inside = at(shift)

        @pl.when(inside)
        def _():
            pl.semaphore_signal(barrier, inc=1, device_id=there, device_id_type=MESH)

    greeted = jnp.int32(0)
    for shift in around:
        greeted = greeted + at(shift)[1].astype(jnp.int32)
    pl.semaphore_wait(barrier, greeted)

    for fetch in fetches[6:] + fetches[:1]:
        fetch.wait()

    def entry_at(turn):
        route = turn // mcap
        turned = jnp.where(route < 2, 1 - route, route)
        return jnp.where(here[2] % 2 == 0, route, turned), turn % mcap

    moved = []
    for turn in range(entries):
        route, k = entry_at(turn)
        moved.append(moves_ref[0, 0, k, route])
    count = jnp.int32(0)
    rank = []
    for entry in moved:
        rank.append(count)
        count = count + (entry >= 0).astype(jnp.int32)
    where_to = []
    for slot in range(slots):
        spot = count
        goes = jnp.int32(0)
        for entry, spot_of in zip(moved, rank):
            spot = jnp.where(entry == slot, spot_of, spot)
            goes = jnp.where(entry == slot, 1, goes)
        count = count + (1 - goes)
        where_to.append(spot)
    for slot in range(slots):
        taken = jnp.int32(0)
        for other in range(slots):
            taken = jnp.where(where_to[other] == slot, other, taken)
        place[0, slot] = taken
        place[1, slot] = where_to[slot]
    for e in range(entries):
        place[2, e] = jnp.minimum(rank[e], slots - 1)

    def speeds(wind, component, x):
        return jnp.stack([speed_at(wind, component, x, y) for y in range(by)])

    def speed_at(wind, component, x, y):
        lane = (y * 2 + component) * bx + x
        return jnp.broadcast_to(wind[:, lane : lane + 1], (bz, bins))

    def gather_faces(slot, load_x):
        wind = state[slot, cells]
        for x in range(bx):
            rows = load_x(x)
            state[slot, pl.ds(x * by, by)] = rows
            for y in range(by):
                floor[slot, x, pl.ds(y, 1), :] = rows[y, 0:1, :]
            for y, side in ((by - 1, 0), (0, 1)):
                speed = speed_at(wind, 1, x, y)
                bounded = jnp.maximum(speed, 0.0) if side == 0 else jnp.minimum(speed, 0.0)
                face_y[side, slot, x] = bounded * rows[y]
            if x == bx - 1:
                face_x[0, slot] = jnp.maximum(speeds(wind, 0, x), 0.0) * rows
            if x == 0:
                face_x[1, slot] = jnp.minimum(speeds(wind, 0, x), 0.0) * rows

    def exchange(turn, sends_ref):
        copies = []
        for side in range(4):
            local, out, got = (
                (face_x, send_x, got_x) if side < 2 else (face_y, send_y, got_y)
            )
            back = opposite[side]
            there, inside = at(side_shift[side])

            def pick(k, carry, side=side, local=local, out=out, back=back):
                entry = sends_ref[0, k, 0, side]
                rows = local[back % 2, jnp.clip(entry, 0, slots - 1)]
                out[turn, side % 2, k] = jnp.where(entry >= 0, rows, 0.0)
                return carry

            lax.fori_loop(0, fcap, pick, 0)
            copy = pltpu.make_async_remote_copy(
                src_ref=out.at[turn, side % 2],
                dst_ref=got[turn].at[back % 2],
                send_sem=face_out.at[turn, side],
                recv_sem=face_in.at[turn, back],
                device_id=there,
                device_id_type=MESH,
            )
            pl.when(inside)(copy.start)
            copies.append((copy, inside))
        return copies

    def floor_copy(turn, slot):
        return pltpu.make_async_remote_copy(
            src_ref=floor.at[slot],
            dst_ref=got_floor[turn].at[slot],
            send_sem=floor_out.at[turn, slot],
            recv_sem=floor_in.at[turn, slot],
            device_id=at((0, 0, -1))[0],
            device_id_type=MESH,
        )

    def send_floor(turn, slot):
        pl.when(at((0, 0, -1))[1])(floor_copy(turn, slot).start)

    def await_faces(turn):
        _, above_inside = at((0, 0, 1))
        for side in range(4):
            _, inside = at(side_shift[side])
            got = got_x if side < 2 else got_y
            landing = pltpu.make_async_remote_copy(
                src_ref=got[turn].at[side % 2],
                dst_ref=got[turn].at[side % 2],
                send_sem=face_out.at[turn, side],
                recv_sem=face_in.at[turn, side],
                device_id=at(side_shift[side])[0],
                device_id_type=MESH,
            )
            pl.when(inside)(landing.wait_recv)

        @pl.when(above_inside)
        def _():
            for slot in range(slots):
                floor_copy(turn, slot).wait_recv()

    def await_sent(turn, copies):
        for copy, inside in copies:
            pl.when(inside)(copy.wait_send)

        @pl.when(at((0, 0, -1))[1])
        def _():
            for slot in range(slots):
                floor_copy(turn, slot).wait_send()

    def step(turn, slot, nb_ref, turns_ref, target, spot):
        wind = state[slot, cells]
        ghosts = []
        for side in range(4):
            local, got = (face_x, got_x) if side < 2 else (face_y, got_y)
            code = nb_ref[0, 0, side, slot]
            near = local[side % 2, jnp.clip(code, 0, slots - 1)]
            far = got[turn][side % 2, jnp.clip(code - slots, 0, fcap - 1)]
            ghosts.append(jnp.where(code < 0, 0.0, jnp.where(code < slots, near, far)))
        west, east, south, north = ghosts
        has_above = here[2] + 1 < peers[2]
        fall = fall_ref[...].reshape(1, 1, bins)
        level = lax.broadcasted_iota(jnp.int32, (by, bz, bins), 1)
        rows = state[slot, pl.ds(0, by)]
        speed = speeds(wind, 0, 0)
        behind = west
        for x in range(bx):
            upward = jnp.maximum(speed, 0.0) * rows
            downward = jnp.minimum(speed, 0.0) * rows
            if x + 1 < bx:
                later = state[slot, pl.ds((x + 1) * by, by)]
                later_speed = speeds(wind, 0, x + 1)
                ahead = jnp.minimum(later_speed, 0.0) * later
            else:
                ahead = east
            total_x = (upward + ahead) - (behind + downward)
            speed_y = speeds(wind, 1, x)
            up_y = jnp.maximum(speed_y, 0.0) * rows
            down_y = jnp.minimum(speed_y, 0.0) * rows
            ahead_y = jnp.concatenate([down_y[1:], north[x][None]], axis=0)
            behind_y = jnp.concatenate([south[x][None], up_y[:-1]], axis=0)
            total_y = (up_y + ahead_y) - (behind_y + down_y)
            top = jnp.stack(
                [
                    jnp.broadcast_to(got_floor[turn][slot, x, pl.ds(y, 1), :], (bz, bins))
                    for y in range(by)
                ]
            )
            top = jnp.where(has_above, top, 0.0)
            upper = jnp.where(level == bz - 1, top, pltpu.roll(rows, bz - 1, 1))
            target[spot, pl.ds(x * by, by)] = rows - total_x - total_y - fall * (rows - upper)
            behind = upward
            if x + 1 < bx:
                rows, speed = later, later_speed
        turns = turns_ref[0, 0, 0, slot]
        size = step_time / jnp.maximum(jnp.full((1, bins), turns, jnp.int32), 1).astype(jnp.float32)

        pieces = 4 if cells % 4 == 0 else 1
        part_cells = cells // pieces
        lead = [
            target[spot, pl.ds(i * part_cells, part_cells)].reshape(part_cells * bz, bins)
            for i in range(pieces)
        ]
        for index in range(most_turns):
            firsts = [product(mass, map_one) for mass in lead]
            lost, seconds = [], []
            for mass, first in zip(lead, firsts):
                parts = [first[:, i * bins : (i + 1) * bins] for i in range(6)]
                lost.append(mass * (parts[2] + parts[5]))
                paired = (parts[0] + parts[3]) * (parts[1] + parts[4])
                seconds.append(product(paired, map_two))
            lead = [
                jnp.where(
                    index < turns,
                    mass + size * (second[:, :bins] + second[:, bins:] - gone),
                    mass,
                )
                for mass, second, gone in zip(lead, seconds, lost)
            ]
        for i in range(pieces):
            target[spot, pl.ds(i * part_cells, part_cells)] = lead[i].reshape(
                part_cells, bz, bins
            )

    def first_faces(slot, carry):
        fetch_mass(slot).wait()
        held = occupied_ref[0, 0, slot] > 0
        columns = wind_ref[0, 0, slot].reshape(2 * bx, by * bz).T
        for y in range(by):
            state[slot, cells, :, pl.ds(y * 2 * bx, 2 * bx)] = columns[y * bz : (y + 1) * bz]
        gather_faces(
            slot, lambda x: jnp.where(held, mass_ref[slot, pl.ds(x * by, by)], 0.0)
        )
        send_floor(0, slot)
        return carry

    lax.fori_loop(0, slots, first_faces, 0)
    copies = exchange(0, old_sends_ref)
    for fetch in fetches[1:6]:
        fetch.wait()
    for i, ref in enumerate((gain_a_ref, gain_b_ref, loss_k_ref)):
        for row in (0, bins):
            for part, values in enumerate(split(ref[...])):
                map_one[pl.ds(row, bins), pl.ds((part * 3 + i) * bins, bins)] = values
    for row in (0, bins):
        for part, values in enumerate(split(gain_c_ref[...])):
            map_two[pl.ds(row, bins), pl.ds(part * bins, bins)] = values
    await_faces(0)

    def move_copy(e):
        route = e // mcap
        west_leg = jnp.where(route == 1, 0, -1)
        north_leg = jnp.where(route == 0, 0, 1)
        there, inside = at((west_leg, north_leg, 0))
        _, incoming = at((-west_leg, -north_leg, 0))
        copy = pltpu.make_async_remote_copy(
            src_ref=parcel.at[e],
            dst_ref=arrived.at[e],
            send_sem=move_out.at[e],
            recv_sem=move_in.at[e],
            device_id=there,
            device_id_type=MESH,
        )
        return copy, inside, incoming

    def post(turn, carry):
        route, k = entry_at(turn)
        e = route * mcap + k
        copy, inside, _ = move_copy(e)
        parcel[e] = done[place[2, turn]]
        pl.when(inside)(copy.start)
        return carry

    def first_step(spot, carry):
        slot = place[0, spot]
        step(0, slot, old_nb_ref, old_turns_ref, done, spot)
        done[spot, cells] = state[slot, cells]
        return carry

    def first_and_post(spot, carry):
        first_step(spot, carry)
        return post(spot, carry)

    shared = min(slots, entries)
    lax.fori_loop(0, shared, first_and_post, 0)
    if slots > shared:
        lax.fori_loop(shared, slots, first_step, 0)
    if entries > shared:
        lax.fori_loop(shared, entries, post, 0)
    await_sent(0, copies)

    def land(e, carry):
        copy, _, incoming = move_copy(e)
        pl.when(incoming)(copy.wait_recv)
        return carry

    lax.fori_loop(0, entries, land, 0)

    def second_faces(slot, carry):
        code = sources_ref[0, 0, slot]
        own = place[1, jnp.clip(code, 0, slots - 1)]
        came = jnp.clip(code - slots, 0, entries - 1)

        def choose(first, length):
            near = done[own, pl.ds(first, length)]
            far = arrived[came, pl.ds(first, length)]
            return jnp.where(code < 0, 0.0, jnp.where(code < slots, near, far))

        state[slot, cells] = choose(cells, 1)[0]
        gather_faces(slot, lambda x: choose(x * by, by))
        send_floor(1, slot)
        return carry

    lax.fori_loop(0, slots, second_faces, 0)
    copies = exchange(1, new_sends_ref)
    await_faces(1)

    def second_step(slot, carry):
        step(1, slot, new_nb_ref, new_turns_ref, final, slot)
        deliver(slot).start()
        return carry

    def deliver(slot):
        return pltpu.make_async_copy(final.at[slot], out_ref.at[slot], delivered.at[slot])

    lax.fori_loop(0, slots, second_step, 0)
    for slot in range(slots):
        deliver(slot).wait()
    await_sent(1, copies)

    def sent(e, carry):
        copy, inside, _ = move_copy(e)
        pl.when(inside)(copy.wait_send)
        return carry

    lax.fori_loop(0, entries, sent, 0)


def on_device(peers, bin_mass, wind_field, fall_speed, *rest):
    slots, bx, by, bz, bins = bin_mass.shape[2:]
    cells = bx * by
    old_sends, move_lists = rest[6], rest[8]
    fcap, mcap = old_sends.shape[-1], move_lists.shape[-1]
    entries = 3 * mcap
    small = [wind_field, fall_speed.reshape(1, bins), *rest]
    for i in (7, 12):
        small[i] = small[i].transpose(0, 1, 3, 2)
    for i in (8, 13):
        small[i] = small[i].transpose(0, 3, 1, 2)
    small[10] = small[10].transpose(0, 1, 3, 2)
    dims = (slots, bx, by, bz, bins, fcap, mcap, peers)
    hbm = pl.BlockSpec(memory_space=pltpu.HBM)
    f32 = jnp.float32
    result = pl.pallas_call(
        functools.partial(kernel, dims),
        out_shape=jax.ShapeDtypeStruct((slots, cells, bz, bins), f32),
        in_specs=[hbm] * 16,
        out_specs=hbm,
        scratch_shapes=[
            pltpu.VMEM((slots, cells, bz, bins), f32),
            *[pltpu.VMEM(array.shape, f32) for array in small[:6]],
            *[pltpu.SMEM(array.shape, jnp.int32) for array in small[6:]],
            pltpu.SemaphoreType.DMA((slots,)),
            pltpu.SemaphoreType.DMA((len(small),)),
            pltpu.VMEM((slots, cells + 1, bz, bins), f32),
            pltpu.VMEM((slots, cells + 1, bz, bins), f32),
            pltpu.VMEM((entries, cells + 1, bz, bins), f32),
            pltpu.VMEM((entries, cells + 1, bz, bins), f32),
            pltpu.VMEM((2, slots, by, bz, bins), f32),
            pltpu.VMEM((2, slots, bx, bz, bins), f32),
            pltpu.VMEM((2, 2, fcap, by, bz, bins), f32),
            pltpu.VMEM((2, 2, fcap, bx, bz, bins), f32),
            pltpu.VMEM((2, fcap, by, bz, bins), f32),
            pltpu.VMEM((2, fcap, by, bz, bins), f32),
            pltpu.VMEM((2, fcap, bx, bz, bins), f32),
            pltpu.VMEM((2, fcap, bx, bz, bins), f32),
            pltpu.VMEM((slots, bx, by, bins), f32),
            pltpu.VMEM((slots, bx, by, bins), f32),
            pltpu.VMEM((slots, bx, by, bins), f32),
            pltpu.VMEM((2 * bins, 6 * bins), jnp.bfloat16),
            pltpu.VMEM((2 * bins, 2 * bins), jnp.bfloat16),
            pltpu.SMEM((3, max(slots, entries)), jnp.int32),
            pltpu.SemaphoreType.DMA((2, 4)),
            pltpu.SemaphoreType.DMA((2, 4)),
            pltpu.SemaphoreType.DMA((2, slots)),
            pltpu.SemaphoreType.DMA((2, slots)),
            pltpu.SemaphoreType.DMA((entries,)),
            pltpu.SemaphoreType.DMA((entries,)),
            pltpu.VMEM((slots, cells, bz, bins), f32),
            pltpu.SemaphoreType.DMA((slots,)),
        ],
        compiler_params=pltpu.CompilerParams(
            collective_id=0, has_side_effects=True, vmem_limit_bytes=56 * 1024 * 1024
        ),
    )(
        bin_mass.reshape(slots, cells, bz, bins),
        *small,
    )
    return result.reshape(bin_mass.shape)


def solution(mesh):
    peers = tuple(mesh.shape[name] for name in ("gx", "gy", "gz"))
    placed = (
        P("gx", "gy", "gz", None, None, None, None),
        P("gx", "gy", "gz", None, None, None),
        P(),
        P(),
        P(),
        P(),
        P(),
        P("gx", "gy", None),
        P("gx", "gy", None, None),
        P("gx", "gy", None, None),
        P(None, "gx", "gy", "gz"),
        P("gx", "gy", None, None),
        P("gx", "gy", None),
        P("gx", "gy", None, None),
        P("gx", "gy", None, None),
        P(None, "gx", "gy", "gz"),
    )
    return jax.shard_map(
        functools.partial(on_device, peers),
        mesh=mesh,
        in_specs=placed,
        out_specs=P("gx", "gy", "gz", None, None, None, None),
        check_vma=False,
    )
```
